128 devices in a mesh: tm: 8 (over z, y_hi), space: 16 (over y_lo, x, core).
Axes of the slice: x: 4, y: 4 (y_hi: 2, y_lo: 2; y = y_hi * 2 + y_lo), z: 4, core: 2. Of those that a mesh axis runs over, the one named last changes fastest.
Arguments:
- right_side: float32 [128, 2048, 128], P('space', 'tm'), may hold values from -3 to 3
- blocks: float32 [128, 7, 128, 128], P('space'), may hold values from -0.1875 to 0.1875
- neighbors: int32 [128, 7], P('space'), may hold values from 0 to 127, as said below
- shift_rates: float32 [4], replicated, may hold values from 5 to 8
Outputs:
- correction: float32 [128, 2048, 128], P('space', 'tm')
The draws below stay inside these ranges and needn't reach their ends.
Inputs may be any that keep to these rules, and one draw needn't show every extreme that they name: The elements form planes of 8 consecutive elements. neighbors[e, 0] = e. With q the plane of e, column 1 names an element of plane q - 1 and column 2 one of plane q + 1, cyclically over the planes; within a plane, each of these two columns names every element of the neighbouring plane exactly once. Columns 3 to 6 name elements of plane q.
All inputs are finite; a program needn't handle non-finite values.
Results may differ from the reference program's by a relative error of at most 0.0003.
Values sent between devices are 32-bit elements; how exact they have to be, the bound alone decides.
No kernel may reach another device: no remote copies, remote signals or barrier semaphores. Data moves between devices by JAX's collectives and lax.ppermute only.
A program may use at most 128 MiB of HBM per device.

```python
import math
import jax
import jax.numpy as jnp
from jax import lax

P_SIZE = 128
L = 2048
E_DEV = 8
SWEEPS = 4
ELEMS = 128


def permuted_row(subkey):
    return jax.random.permutation(subkey, E_DEV)


def draw_neighbors(key, part):
    plane_count = ELEMS // E_DEV
    element = jnp.arange(ELEMS, dtype=jnp.int32)
    plane_of = element // E_DEV
    subkeys = jax.random.split(jax.random.fold_in(key, 11), 2 * plane_count)
    shuffles = jax.vmap(permuted_row)(subkeys).astype(jnp.int32)
    before = shuffles[:plane_count].reshape(-1)
    after = shuffles[plane_count:].reshape(-1)
    prev_plane = (plane_of - 1) % plane_count
    next_plane = (plane_of + 1) % plane_count
    column_before = prev_plane * E_DEV + before
    column_after = next_plane * E_DEV + after
    inside = jax.random.randint(jax.random.fold_in(key, 12), (ELEMS, 4), 0, E_DEV, dtype=jnp.int32)
    inside = inside + (plane_of * E_DEV)[:, None]
    return jnp.concatenate([element[:, None], column_before[:, None], column_after[:, None], inside], 1)


def levels(rng, shape, shards, smallest, top_value):
    def one(position, parts):
        draws = jax.random.uniform(jax.random.fold_in(jax.random.fold_in(rng, 6), position), (parts,), jnp.float32, smallest / len(shards), top_value / len(shards))
        return jnp.repeat(jnp.exp(draws), shape[position] // parts).reshape((-1,) + (1,) * (len(shape) - position - 1))

    factor_of = one(*shards[0])
    for cut in shards[1:]:
        factor_of = factor_of * one(*cut)
    return factor_of


def gaussian(stream_key, shape, scale, limit, cuts=(), kind=jnp.bfloat16):
    entries = scale * jax.random.normal(stream_key, shape, jnp.float32)
    if cuts:
        entries = entries * levels(stream_key, shape, cuts, -0.22, 0.18)
    return jnp.clip(entries, -limit, limit).astype(kind)


def setup_inputs(seed: int = 0) -> dict:
    key_list = jax.random.split(jax.random.key(seed), 5)
    return {
        "right_side": gaussian(key_list[0], (ELEMS, L, P_SIZE), 0.5, 3.0, ((0, 16), (1, 8)), jnp.float32),
        "blocks": gaussian(key_list[1], (ELEMS, 7, P_SIZE, P_SIZE), (7 * P_SIZE) ** -0.5, 0.1875, ((0, 16),), jnp.float32),
        "neighbors": draw_neighbors(jax.random.fold_in(key_list[4], 71), 0),
        "shift_rates": jnp.clip(jax.random.uniform(key_list[3], (SWEEPS,), jnp.float32, 5.0, 8.0), 5.0, 8.0),
    }


WRAP_WEIGHT = 0.01
DIAG_WEIGHT = 6.0
BLOCK_WEIGHT = 3.0
STEP_SCALE = 0.1
EXACT_DOTS = lax.Precision.HIGHEST


def apply_operator(values, blocks, neighbors):
    def add_slot(slot_index, running):
        taken = jnp.take(values, neighbors[:, slot_index], axis=0)
        matrix = lax.dynamic_index_in_dim(blocks, slot_index, 1, keepdims=False)
        return running + jnp.einsum("eij,elj->eli", matrix, taken, precision=EXACT_DOTS)

    summed = lax.fori_loop(0, 7, add_slot, jnp.zeros_like(values))
    return STEP_SCALE * (DIAG_WEIGHT * values + BLOCK_WEIGHT * summed)


def reference(right_side, blocks, neighbors, shift_rates):
    moments = jnp.arange(L).astype(jnp.float32)
    growth = jnp.exp(moments * (math.log(WRAP_WEIGHT) / L))
    scaled = right_side * growth[None, :, None]
    spectrum = jnp.fft.fft(scaled, axis=1)
    spec_real = jnp.real(spectrum).astype(jnp.float32)
    spec_imag = jnp.imag(spectrum).astype(jnp.float32)
    decay_root = math.exp(math.log(WRAP_WEIGHT) / L)
    phases = moments * (2.0 * math.pi / L)
    shift_real = (1.0 - decay_root * jnp.cos(phases))[None, :, None]
    shift_imag = (decay_root * jnp.sin(phases))[None, :, None]
    iter_real = jnp.zeros_like(spec_real)
    iter_imag = jnp.zeros_like(spec_real)
    for sweep_index in range(SWEEPS):
        if sweep_index == 0:
            res_real = spec_real
            res_imag = spec_imag
        else:
            res_real = spec_real - (shift_real * iter_real - shift_imag * iter_imag) - apply_operator(iter_real, blocks, neighbors)
            res_imag = spec_imag - (shift_real * iter_imag + shift_imag * iter_real) - apply_operator(iter_imag, blocks, neighbors)
        den_real = shift_real + STEP_SCALE * shift_rates[sweep_index]
        den_imag = shift_imag
        magnitude = den_real * den_real + den_imag * den_imag
        inv_real = den_real / magnitude
        inv_imag = -den_imag / magnitude
        iter_real, iter_imag = (iter_real + inv_real * res_real - inv_imag * res_imag,
                                iter_imag + inv_real * res_imag + inv_imag * res_real)
    returned = jnp.fft.ifft(lax.complex(iter_real, iter_imag), axis=1)
    return jnp.real(returned) / growth[None, :, None]
```

```python
import functools
import math

import jax
import jax.numpy as jnp
import numpy as np
from jax import lax
from jax.experimental import pallas as pl
from jax.experimental.pallas import tpu as pltpu
from jax.sharding import PartitionSpec as P

SWEEPS = 4
LENGTH = 2048
CLASSES = 8
HALF = 128
NODES = 128
PLANE = 8
WRAP_WEIGHT = 0.01
DIAG_WEIGHT = 6.0
BLOCK_WEIGHT = 3.0
STEP_SCALE = 0.1
INNER_SLOTS = (0, 3, 4, 5, 6)
ROOT2 = math.sqrt(0.5)
VMEM_LIMIT = 48 * 1024 * 1024


def slot_frequencies(c):
    j = np.arange(HALF)
    return 8 * j if c == 0 else c + 16 * j


def transform_tables():
    m = np.arange(HALF)
    log_g = math.log(WRAP_WEIGHT) / LENGTH
    forward = np.zeros((CLASSES, 256, 256))
    inverse = np.zeros((CLASSES, 256, 256))
    for c in range(CLASSES):
        k = slot_frequencies(c)
        angle = 2.0 * np.pi * ((k[:, None] * m[None, :]) % LENGTH) / LENGTH
        cos, sin = np.cos(angle), np.sin(angle)
        if c:
            forward[c] = np.block([[cos, sin], [-sin, cos]])
            inverse[c] = np.block([[cos.T, -sin.T], [sin.T, cos.T]]) * (2.0 / LENGTH)
        else:
            even = (np.arange(HALF) % 2 == 0)[:, None]
            sign = np.where(m % 2 == 0, 1.0, -1.0)
            cos_even, cos_odd = cos * even, cos * ~even
            sin_even, sin_odd = sin * even, sin * ~even
            forward[c] = np.block([[cos_even, cos_odd], [-sin_even, -sin_odd]])
            forward[c, HALF, :HALF] = sign
            back = np.block([[cos_even.T, -sin_even.T], [cos_odd.T, -sin_odd.T]]) * (2.0 / LENGTH)
            back[:HALF, 0] = 1.0 / LENGTH
            back[:HALF, HALF] = sign / LENGTH
            inverse[c] = back
    growth = np.exp(log_g * m)
    forward *= np.tile(growth, 2)[None, None, :]
    inverse /= np.tile(growth, 2)[None, :, None]
    return forward, inverse


def shift_table():
    root = math.exp(math.log(WRAP_WEIGHT) / LENGTH)
    table = np.zeros((CLASSES, 3, HALF, NODES))
    for c in range(CLASSES):
        angle = 2.0 * np.pi * slot_frequencies(c) / LENGTH
        real = 1.0 - root * np.cos(angle)
        second = real.copy()
        if c == 0:
            second[0] = 1.0 + root
        table[c, 0] = real[:, None]
        table[c, 1] = second[:, None]
        table[c, 2] = (root * np.sin(angle))[:, None]
    return table.astype(np.float32)


def split_host(matrix):
    high = matrix.astype(jnp.bfloat16)
    low = (matrix - high.astype(np.float64)).astype(jnp.bfloat16)
    return high, low


def split(value):
    high = value.astype(jnp.bfloat16)
    return high, (value - high.astype(jnp.float32)).astype(jnp.bfloat16)


def dot(a, b):
    return jnp.dot(a, b, preferred_element_type=jnp.float32)


BLOCK_GROWTH = [math.exp(math.log(WRAP_WEIGHT) * q / 16.0) for q in range(16)]


def real_dft16(s):
    u = [s[r] + s[r + 8] for r in range(8)]
    w = [s[r] - s[r + 8] for r in range(8)]
    p = [u[r] + u[r + 4] for r in range(4)]
    t = [u[r] - u[r + 4] for r in range(4)]
    out = [None] * 8
    a, b = p[0] + p[2], p[1] + p[3]
    out[0] = (a + b, a - b)
    out[4] = (p[0] - p[2], p[3] - p[1])
    minus, plus = ROOT2 * (t[1] - t[3]), ROOT2 * (t[1] + t[3])
    out[2] = (t[0] + minus, -t[2] - plus)
    out[6] = (t[0] - minus, t[2] - plus)
    lower = [w[r] - w[8 - r] for r in (1, 2, 3)]
    upper = [w[r] + w[8 - r] for r in (1, 2, 3)]
    for c in (1, 3, 5, 7):
        real = w[0]
        imag = -w[4] if c % 4 == 1 else w[4]
        for r in (1, 2, 3):
            real = real + math.cos(math.pi * c * r / 8) * lower[r - 1]
            imag = imag - math.sin(math.pi * c * r / 8) * upper[r - 1]
        out[c] = (real, imag)
    return out


def real_idft16(v):
    (v0, v8), (r2, i2), (r4, i4), (r6, i6) = v[0], v[2], v[4], v[6]
    a, b = v0 + v8, v0 - v8
    ee = [a + r4, b - i4, a - r4, b + i4]
    x, y = r2 - r6, i2 + i6
    eo = [r2 + r6, ROOT2 * (x - y), i6 - i2, -ROOT2 * (x + y)]
    even = [ee[q] + eo[q] for q in range(4)] + [ee[q] - eo[q] for q in range(4)]
    odd = [None] * 8
    odd[0] = (v[1][0] + v[3][0]) + (v[5][0] + v[7][0])
    odd[4] = (v[3][1] - v[1][1]) + (v[7][1] - v[5][1])
    for q in (1, 2, 3):
        real = sum(math.cos(math.pi * c * q / 8) * v[c][0] for c in (1, 3, 5, 7))
        imag = sum(math.sin(math.pi * c * q / 8) * v[c][1] for c in (1, 3, 5, 7))
        odd[q] = real - imag
        odd[8 - q] = -real - imag
    return [even[q] + odd[q] for q in range(8)] + [even[q] - odd[q] for q in range(8)]


CHUNK = 16


def forward_kernel(x_ref, high_ref, low_ref, out_ref, z_ref):
    @pl.loop(0, HALF // CHUNK)
    def _(step):
        row = pl.multiple_of(step * CHUNK, CHUNK)
        series = [
            x_ref[q // 2, pl.ds(q % 2 * HALF + row, CHUNK), :] * BLOCK_GROWTH[q] for q in range(16)
        ]
        for c, pair in enumerate(real_dft16(series)):
            for part in range(2):
                high, low = split(pair[part])
                z_ref[c, pl.ds(part * HALF + row, CHUNK), :NODES] = high
                z_ref[c, pl.ds(part * HALF + row, CHUNK), NODES:] = low

    for c in range(CLASSES):
        both = dot(high_ref[c], z_ref[c])
        out_ref[c] = both[:, :NODES] + both[:, NODES:] + dot(low_ref[c], z_ref[c, :, :NODES])


def inverse_kernel(y_ref, high_ref, low_ref, out_ref, v_ref):
    for c in range(CLASSES):
        high, low = split(y_ref[c])
        both = dot(high_ref[c], jnp.concatenate([high, low], 1))
        v_ref[c] = both[:, :NODES] + both[:, NODES:] + dot(low_ref[c], high)

    @pl.loop(0, HALF // CHUNK)
    def _(step):
        row = pl.multiple_of(step * CHUNK, CHUNK)
        pairs = [
            (v_ref[c, pl.ds(row, CHUNK), :], v_ref[c, pl.ds(HALF + row, CHUNK), :])
            for c in range(CLASSES)
        ]
        for q, value in enumerate(real_idft16(pairs)):
            out_ref[q // 2, pl.ds(q % 2 * HALF + row, CHUNK), :] = value * (1.0 / BLOCK_GROWTH[q])


def weights_kernel(blocks_ref, inner_ref, rim_ref):
    for e in range(PLANE):
        for target, slots in ((inner_ref, INNER_SLOTS), (rim_ref, (1, 2))):
            for place, s in enumerate(slots):
                high, low = split(blocks_ref[e, s].T)
                target[e, place * NODES : (place + 1) * NODES, :NODES] = high
                target[e, place * NODES : (place + 1) * NODES, NODES:] = low


def solved(shift_ref, shift):
    first = shift_ref[0] + shift
    second = shift_ref[1] + shift
    imaginary = shift_ref[2]
    scale = 1.0 / (first * second + imaginary * imaginary)
    a, b, c = second * scale, imaginary * scale, first * scale
    return lambda real, imag: (a * real + b * imag, c * imag - b * real)


def first_kernel(rates_ref, spec_ref, shift_ref, out_ref):
    apply = solved(shift_ref, STEP_SCALE * rates_ref[0])

    @pl.loop(0, PLANE)
    def _(e):
        real, imag = apply(spec_ref[e, :HALF], spec_ref[e, HALF:])
        out_ref[e, :HALF] = real
        out_ref[e, HALF:] = imag


def inner_kernel(nb_ref, y_ref, weights_ref, out_ref, high_ref, low_ref):
    @pl.loop(0, PLANE)
    def _(e):
        high_ref[e], low_ref[e] = split(y_ref[e])

    @pl.loop(0, PLANE)
    def _(e):
        picked = [nb_ref[e, s] % PLANE for s in INNER_SLOTS]
        high = jnp.concatenate([high_ref[i] for i in picked], 1)
        low = jnp.concatenate([low_ref[i] for i in picked], 1)
        both = dot(high, weights_ref[e])
        out_ref[e] = both[:, :NODES] + both[:, NODES:] + dot(low, weights_ref[e, :, :NODES])


def rim_kernel(
    sweep, rates_ref, nb_ref, y_ref, inner_ref, before_ref, after_ref, spec_ref, shift_ref, weights_ref, out_ref
):
    shift = STEP_SCALE * rates_ref[sweep]
    apply = solved(shift_ref, shift)

    @pl.loop(0, PLANE)
    def _(e):
        before = before_ref[nb_ref[e, 1] % PLANE]
        after = after_ref[nb_ref[e, 2] % PLANE]
        high, low = split(jnp.concatenate([before, after], 1))
        both = dot(high, weights_ref[e])
        rim = both[:, :NODES] + both[:, NODES:] + dot(low, weights_ref[e, :, :NODES])
        right = (
            spec_ref[e]
            + (shift - STEP_SCALE * DIAG_WEIGHT) * y_ref[e]
            - (STEP_SCALE * BLOCK_WEIGHT) * (inner_ref[e] + rim)
        )
        real, imag = apply(right[:HALF], right[HALF:])
        out_ref[e, :HALF] = real
        out_ref[e, HALF:] = imag


def whole(count):
    return [pl.BlockSpec(memory_space=pltpu.VMEM)] * count


def scalars(count):
    return [pl.BlockSpec(memory_space=pltpu.SMEM)] * count


def call(kernel, outs, specs, flops, moved, scratch=()):
    return pl.pallas_call(
        kernel,
        out_shape=outs,
        in_specs=specs,
        out_specs=jax.tree.map(lambda _: pl.BlockSpec(memory_space=pltpu.VMEM), outs),
        scratch_shapes=scratch,
        compiler_params=pltpu.CompilerParams(vmem_limit_bytes=VMEM_LIMIT),
        cost_estimate=pl.CostEstimate(flops=flops, bytes_accessed=moved, transcendentals=0),
    )


STATE = jax.ShapeDtypeStruct((PLANE, 2 * HALF, NODES), jnp.float32)
MIB = 1 << 20


def per_device(right_side, blocks, neighbors, shift_rates):
    forward, inverse = transform_tables()
    forward_high, forward_low = (jnp.asarray(part) for part in split_host(forward))
    inverse_high, inverse_low = (jnp.asarray(part) for part in split_host(inverse))
    shifts = lax.dynamic_index_in_dim(
        jnp.asarray(shift_table()), lax.axis_index("tm"), 0, keepdims=False
    )
    ring = lax.axis_size("space")
    up = [(i, (i + 1) % ring) for i in range(ring)]
    down = [(j, i) for i, j in up]

    def exchange(value):
        return lax.all_to_all(value, "tm", 0, 0, tiled=True)

    inner_weights, rim_weights = call(
        weights_kernel,
        (
            jax.ShapeDtypeStruct((PLANE, 5 * NODES, 2 * NODES), jnp.bfloat16),
            jax.ShapeDtypeStruct((PLANE, 2 * NODES, 2 * NODES), jnp.bfloat16),
        ),
        whole(1),
        0,
        8 * MIB,
    )(blocks)
    steps = exchange(right_side)
    spectrum = call(
        forward_kernel,
        STATE,
        whole(3),
        10**9,
        4 * MIB,
        [pltpu.VMEM((CLASSES, 256, 256), jnp.bfloat16)],
    )(steps, forward_high, forward_low)
    spectrum = exchange(spectrum)
    state = call(first_kernel, STATE, scalars(1) + whole(2), 0, 2 * MIB)(
        shift_rates, spectrum, shifts
    )
    for sweep in range(1, SWEEPS):
        before = lax.ppermute(state, "space", up)
        after = lax.ppermute(state, "space", down)
        inner = call(
            inner_kernel,
            STATE,
            scalars(1) + whole(2),
            2 * 10**9,
            5 * MIB,
            [pltpu.VMEM((PLANE, 2 * HALF, NODES), jnp.bfloat16)] * 2,
        )(neighbors, state, inner_weights)
        state = call(
            functools.partial(rim_kernel, sweep),
            STATE,
            scalars(2) + whole(7),
            10**9,
            7 * MIB,
        )(shift_rates, neighbors, state, inner, before, after, spectrum, shifts, rim_weights)
    steps = call(
        inverse_kernel,
        STATE,
        whole(3),
        10**9,
        4 * MIB,
        [pltpu.VMEM((CLASSES, 256, 128), jnp.float32)],
    )(exchange(state), inverse_high, inverse_low)
    return exchange(steps)


def solution(mesh):
    return jax.shard_map(
        per_device,
        mesh=mesh,
        in_specs=(P("space", "tm", None), P("space", None, None, None), P("space", None), P()),
        out_specs=P("space", "tm", None),
        check_vma=False,
    )
```

```python
import functools
import math

import jax
import jax.numpy as jnp
import numpy as np
from jax import lax
from jax.experimental import pallas as pl
from jax.experimental.pallas import tpu as pltpu
from jax.sharding import PartitionSpec as P

SWEEPS = 4
LENGTH = 2048
CLASSES = 8
HALF = 128
PARTS = 2
SLOTS = HALF // PARTS
ROWS = 2 * SLOTS
NODES = 128
PLANE = 8
WRAP_WEIGHT = 0.01
DIAG_WEIGHT = 6.0
BLOCK_WEIGHT = 3.0
STEP_SCALE = 0.1
INNER_SLOTS = (0, 3, 4, 5, 6)
ROOT2 = math.sqrt(0.5)
VMEM_LIMIT = 48 * 1024 * 1024


def slot_frequencies(c):
    j = np.arange(HALF)
    return 8 * j if c == 0 else c + 16 * j


def transform_tables():
    m = np.arange(HALF)
    log_g = math.log(WRAP_WEIGHT) / LENGTH
    forward = np.zeros((CLASSES, 256, 256))
    inverse = np.zeros((CLASSES, 256, 256))
    for c in range(CLASSES):
        k = slot_frequencies(c)
        angle = 2.0 * np.pi * ((k[:, None] * m[None, :]) % LENGTH) / LENGTH
        cos, sin = np.cos(angle), np.sin(angle)
        if c:
            forward[c] = np.block([[cos, sin], [-sin, cos]])
            inverse[c] = np.block([[cos.T, -sin.T], [sin.T, cos.T]]) * (2.0 / LENGTH)
        else:
            even = (np.arange(HALF) % 2 == 0)[:, None]
            sign = np.where(m % 2 == 0, 1.0, -1.0)
            cos_even, cos_odd = cos * even, cos * ~even
            sin_even, sin_odd = sin * even, sin * ~even
            forward[c] = np.block([[cos_even, cos_odd], [-sin_even, -sin_odd]])
            forward[c, HALF, :HALF] = sign
            back = np.block([[cos_even.T, -sin_even.T], [cos_odd.T, -sin_odd.T]]) * (2.0 / LENGTH)
            back[:HALF, 0] = 1.0 / LENGTH
            back[:HALF, HALF] = sign / LENGTH
            inverse[c] = back
    growth = np.exp(log_g * m)
    forward *= np.tile(growth, 2)[None, None, :]
    inverse /= np.tile(growth, 2)[None, :, None]
    order = np.arange(256).reshape(2, PARTS, SLOTS).transpose(1, 0, 2).reshape(256)
    return forward[:, order], inverse[:, :, order]


def shift_table():
    root = math.exp(math.log(WRAP_WEIGHT) / LENGTH)
    table = np.zeros((CLASSES, 3, HALF, NODES))
    for c in range(CLASSES):
        angle = 2.0 * np.pi * slot_frequencies(c) / LENGTH
        real = 1.0 - root * np.cos(angle)
        second = real.copy()
        if c == 0:
            second[0] = 1.0 + root
        table[c, 0] = real[:, None]
        table[c, 1] = second[:, None]
        table[c, 2] = (root * np.sin(angle))[:, None]
    table = table.reshape(CLASSES, 3, PARTS, SLOTS, NODES).transpose(0, 2, 1, 3, 4)
    return table.astype(np.float32)


def split_host(matrix):
    high = matrix.astype(jnp.bfloat16)
    low = (matrix - high.astype(np.float64)).astype(jnp.bfloat16)
    return high, low


def split(value):
    high = value.astype(jnp.bfloat16)
    return high, (value - high.astype(jnp.float32)).astype(jnp.bfloat16)


def dot(a, b):
    return jnp.dot(a, b, preferred_element_type=jnp.float32)


BLOCK_GROWTH = [math.exp(math.log(WRAP_WEIGHT) * q / 16.0) for q in range(16)]


def real_dft16(s):
    u = [s[r] + s[r + 8] for r in range(8)]
    w = [s[r] - s[r + 8] for r in range(8)]
    p = [u[r] + u[r + 4] for r in range(4)]
    t = [u[r] - u[r + 4] for r in range(4)]
    out = [None] * 8
    a, b = p[0] + p[2], p[1] + p[3]
    out[0] = (a + b, a - b)
    out[4] = (p[0] - p[2], p[3] - p[1])
    minus, plus = ROOT2 * (t[1] - t[3]), ROOT2 * (t[1] + t[3])
    out[2] = (t[0] + minus, -t[2] - plus)
    out[6] = (t[0] - minus, t[2] - plus)
    lower = [w[r] - w[8 - r] for r in (1, 2, 3)]
    upper = [w[r] + w[8 - r] for r in (1, 2, 3)]
    for c in (1, 3, 5, 7):
        real = w[0]
        imag = -w[4] if c % 4 == 1 else w[4]
        for r in (1, 2, 3):
            real = real + math.cos(math.pi * c * r / 8) * lower[r - 1]
            imag = imag - math.sin(math.pi * c * r / 8) * upper[r - 1]
        out[c] = (real, imag)
    return out


def real_idft16(v):
    (v0, v8), (r2, i2), (r4, i4), (r6, i6) = v[0], v[2], v[4], v[6]
    a, b = v0 + v8, v0 - v8
    ee = [a + r4, b - i4, a - r4, b + i4]
    x, y = r2 - r6, i2 + i6
    eo = [r2 + r6, ROOT2 * (x - y), i6 - i2, -ROOT2 * (x + y)]
    even = [ee[q] + eo[q] for q in range(4)] + [ee[q] - eo[q] for q in range(4)]
    odd = [None] * 8
    odd[0] = (v[1][0] + v[3][0]) + (v[5][0] + v[7][0])
    odd[4] = (v[3][1] - v[1][1]) + (v[7][1] - v[5][1])
    for q in (1, 2, 3):
        real = sum(math.cos(math.pi * c * q / 8) * v[c][0] for c in (1, 3, 5, 7))
        imag = sum(math.sin(math.pi * c * q / 8) * v[c][1] for c in (1, 3, 5, 7))
        odd[q] = real - imag
        odd[8 - q] = -real - imag
    return [even[q] + odd[q] for q in range(8)] + [even[q] - odd[q] for q in range(8)]


CHUNK = 16


def forward_kernel(x_ref, high_ref, low_ref, *rest):
    out_refs, z_ref = rest[:PARTS], rest[PARTS]

    @pl.loop(0, HALF // CHUNK)
    def _(step):
        row = pl.multiple_of(step * CHUNK, CHUNK)
        series = [
            x_ref[q // 2, pl.ds(q % 2 * HALF + row, CHUNK), :] * BLOCK_GROWTH[q] for q in range(16)
        ]
        for c, pair in enumerate(real_dft16(series)):
            for part in range(2):
                high, low = split(pair[part])
                z_ref[c, pl.ds(part * HALF + row, CHUNK), :NODES] = high
                z_ref[c, pl.ds(part * HALF + row, CHUNK), NODES:] = low

    for c in range(CLASSES):
        both = dot(high_ref[c], z_ref[c])
        result = both[:, :NODES] + both[:, NODES:] + dot(low_ref[c], z_ref[c, :, :NODES])
        for part in range(PARTS):
            out_refs[part][c] = result[part * ROWS : (part + 1) * ROWS]


def inverse_kernel(*refs):
    y_refs = refs[:PARTS]
    high_ref, low_ref, out_ref, v_ref = refs[PARTS:]
    for c in range(CLASSES):
        high, low = split(jnp.concatenate([y_ref[c] for y_ref in y_refs], 0))
        both = dot(high_ref[c], jnp.concatenate([high, low], 1))
        v_ref[c] = both[:, :NODES] + both[:, NODES:] + dot(low_ref[c], high)

    @pl.loop(0, HALF // CHUNK)
    def _(step):
        row = pl.multiple_of(step * CHUNK, CHUNK)
        pairs = [
            (v_ref[c, pl.ds(row, CHUNK), :], v_ref[c, pl.ds(HALF + row, CHUNK), :])
            for c in range(CLASSES)
        ]
        for q, value in enumerate(real_idft16(pairs)):
            out_ref[q // 2, pl.ds(q % 2 * HALF + row, CHUNK), :] = value * (1.0 / BLOCK_GROWTH[q])


def weights_kernel(blocks_ref, inner_ref, rim_ref):
    for e in range(PLANE):
        for target, slots in ((inner_ref, INNER_SLOTS), (rim_ref, (1, 2))):
            for place, s in enumerate(slots):
                high, low = split(blocks_ref[e, s].T)
                target[e, place * NODES : (place + 1) * NODES, :NODES] = high
                target[e, place * NODES : (place + 1) * NODES, NODES:] = low


def solved(shift_ref, part, shift):
    first = shift_ref[part, 0] + shift
    second = shift_ref[part, 1] + shift
    imaginary = shift_ref[part, 2]
    scale = 1.0 / (first * second + imaginary * imaginary)
    a, b, c = second * scale, imaginary * scale, first * scale
    return lambda real, imag: (a * real + b * imag, c * imag - b * real)


def first_kernel(part, rates_ref, spec_ref, shift_ref, out_ref):
    apply = solved(shift_ref, part, STEP_SCALE * rates_ref[0])

    @pl.loop(0, PLANE)
    def _(e):
        real, imag = apply(spec_ref[e, :SLOTS], spec_ref[e, SLOTS:])
        out_ref[e, :SLOTS] = real
        out_ref[e, SLOTS:] = imag


def inner_kernel(nb_ref, y_ref, weights_ref, out_ref, high_ref, low_ref):
    for e in range(PLANE):
        high_ref[e], low_ref[e] = split(y_ref[e])

    @pl.loop(0, PLANE)
    def _(e):
        picked = [nb_ref[e, s] % PLANE for s in INNER_SLOTS]
        high = jnp.concatenate([high_ref[i] for i in picked], 1)
        low = jnp.concatenate([low_ref[i] for i in picked], 1)
        both = dot(high, weights_ref[e])
        out_ref[e] = both[:, :NODES] + both[:, NODES:] + dot(low, weights_ref[e, :, :NODES])


def rim_kernel(
    part,
    sweep,
    rates_ref,
    nb_ref,
    y_ref,
    inner_ref,
    before_ref,
    after_ref,
    spec_ref,
    shift_ref,
    weights_ref,
    out_ref,
):
    shift = STEP_SCALE * rates_ref[sweep]
    apply = solved(shift_ref, part, shift)

    @pl.loop(0, PLANE)
    def _(e):
        before = before_ref[nb_ref[e, 1] % PLANE]
        after = after_ref[nb_ref[e, 2] % PLANE]
        high, low = split(jnp.concatenate([before, after], 1))
        both = dot(high, weights_ref[e])
        rim = both[:, :NODES] + both[:, NODES:] + dot(low, weights_ref[e, :, :NODES])
        right = (
            spec_ref[e]
            + (shift - STEP_SCALE * DIAG_WEIGHT) * y_ref[e]
            - (STEP_SCALE * BLOCK_WEIGHT) * (inner_ref[e] + rim)
        )
        real, imag = apply(right[:SLOTS], right[SLOTS:])
        out_ref[e, :SLOTS] = real
        out_ref[e, SLOTS:] = imag


def whole(count):
    return [pl.BlockSpec(memory_space=pltpu.VMEM)] * count


def scalars(count):
    return [pl.BlockSpec(memory_space=pltpu.SMEM)] * count


def call(kernel, outs, specs, flops, moved, scratch=()):
    return pl.pallas_call(
        kernel,
        out_shape=outs,
        in_specs=specs,
        out_specs=jax.tree.map(lambda _: pl.BlockSpec(memory_space=pltpu.VMEM), outs),
        scratch_shapes=scratch,
        compiler_params=pltpu.CompilerParams(vmem_limit_bytes=VMEM_LIMIT),
        cost_estimate=pl.CostEstimate(flops=flops, bytes_accessed=moved, transcendentals=0),
    )


STEPS = jax.ShapeDtypeStruct((PLANE, 2 * HALF, NODES), jnp.float32)
STATE = jax.ShapeDtypeStruct((PLANE, ROWS, NODES), jnp.float32)
MIB = 1 << 20


def per_device(right_side, blocks, neighbors, shift_rates):
    forward, inverse = transform_tables()
    forward_high, forward_low = (jnp.asarray(part) for part in split_host(forward))
    inverse_high, inverse_low = (jnp.asarray(part) for part in split_host(inverse))
    shifts = lax.dynamic_index_in_dim(
        jnp.asarray(shift_table()), lax.axis_index("tm"), 0, keepdims=False
    )
    ring = lax.axis_size("space")
    up = [(i, (i + 1) % ring) for i in range(ring)]
    down = [(j, i) for i, j in up]

    def exchange(value):
        return lax.all_to_all(value, "tm", 0, 0, tiled=True)

    inner_weights, rim_weights = call(
        weights_kernel,
        (
            jax.ShapeDtypeStruct((PLANE, 5 * NODES, 2 * NODES), jnp.bfloat16),
            jax.ShapeDtypeStruct((PLANE, 2 * NODES, 2 * NODES), jnp.bfloat16),
        ),
        whole(1),
        0,
        8 * MIB,
    )(blocks)
    steps = exchange(right_side)
    steps, inner_weights, rim_weights, shifts = lax.optimization_barrier(
        (steps, inner_weights, rim_weights, shifts)
    )
    spectrum = call(
        forward_kernel,
        (STATE,) * PARTS,
        whole(3),
        10**9,
        4 * MIB,
        [pltpu.VMEM((CLASSES, 256, 256), jnp.bfloat16)],
    )(steps, forward_high, forward_low)
    spectrum = [exchange(part) for part in spectrum]
    states = [
        call(functools.partial(first_kernel, part), STATE, scalars(1) + whole(2), 0, 2 * MIB // PARTS)(
            shift_rates, spectrum[part], shifts
        )
        for part in range(PARTS)
    ]
    for sweep in range(1, SWEEPS):
        for part in range(PARTS):
            state = states[part]
            before = lax.ppermute(state, "space", up)
            after = lax.ppermute(state, "space", down)
            inner = call(
                inner_kernel,
                STATE,
                scalars(1) + whole(2),
                2 * 10**9 // PARTS,
                5 * MIB // PARTS,
                [pltpu.VMEM((PLANE, ROWS, NODES), jnp.bfloat16)] * 2,
            )(neighbors, state, inner_weights)
            states[part] = call(
                functools.partial(rim_kernel, part, sweep),
                STATE,
                scalars(2) + whole(7),
                10**9 // PARTS,
                7 * MIB // PARTS,
            )(
                shift_rates,
                neighbors,
                state,
                inner,
                before,
                after,
                spectrum[part],
                shifts,
                rim_weights,
            )
    steps = call(
        inverse_kernel,
        STEPS,
        whole(PARTS + 2),
        10**9,
        4 * MIB,
        [pltpu.VMEM((CLASSES, 256, 128), jnp.float32)],
    )(*[exchange(state) for state in states], inverse_high, inverse_low)
    return exchange(steps)


def solution(mesh):
    return jax.shard_map(
        per_device,
        mesh=mesh,
        in_specs=(P("space", "tm", None), P("space", None, None, None), P("space", None), P()),
        out_specs=P("space", "tm", None),
        check_vma=False,
    )
```

```python
import functools
import math

import jax
import jax.numpy as jnp
import numpy as np
from jax import lax
from jax.experimental import pallas as pl
from jax.experimental.pallas import tpu as pltpu
from jax.sharding import PartitionSpec as P

SWEEPS = 4
LENGTH = 2048
CLASSES = 8
HALF = 128
PARTS = 2
SLOTS = HALF // PARTS
ROWS = 2 * SLOTS
NODES = 128
PLANE = 8
WRAP_WEIGHT = 0.01
DIAG_WEIGHT = 6.0
BLOCK_WEIGHT = 3.0
STEP_SCALE = 0.1
OWN_SLOTS = (0, 3, 4, 5, 6)
ROOT2 = math.sqrt(0.5)
VMEM_LIMIT = 16 * 1024 * 1024


def slot_frequencies(c):
    j = np.arange(HALF)
    return 8 * j if c == 0 else c + 16 * j


def transform_tables():
    m = np.arange(HALF)
    log_g = math.log(WRAP_WEIGHT) / LENGTH
    forward = np.zeros((CLASSES, 256, 256))
    inverse = np.zeros((CLASSES, 256, 256))
    for c in range(CLASSES):
        k = slot_frequencies(c)
        angle = 2.0 * np.pi * ((k[:, None] * m[None, :]) % LENGTH) / LENGTH
        cos, sin = np.cos(angle), np.sin(angle)
        if c:
            forward[c] = np.block([[cos, sin], [-sin, cos]])
            inverse[c] = np.block([[cos.T, -sin.T], [sin.T, cos.T]]) * (2.0 / LENGTH)
        else:
            even = (np.arange(HALF) % 2 == 0)[:, None]
            sign = np.where(m % 2 == 0, 1.0, -1.0)
            cos_even, cos_odd = cos * even, cos * ~even
            sin_even, sin_odd = sin * even, sin * ~even
            forward[c] = np.block([[cos_even, cos_odd], [-sin_even, -sin_odd]])
            forward[c, HALF, :HALF] = sign
            back = np.block([[cos_even.T, -sin_even.T], [cos_odd.T, -sin_odd.T]]) * (2.0 / LENGTH)
            back[:HALF, 0] = 1.0 / LENGTH
            back[:HALF, HALF] = sign / LENGTH
            inverse[c] = back
    growth = np.exp(log_g * m)
    forward *= np.tile(growth, 2)[None, None, :]
    inverse /= np.tile(growth, 2)[None, :, None]
    order = np.arange(256).reshape(2, PARTS, SLOTS).transpose(1, 0, 2).reshape(256)
    return forward[:, order], inverse[:, :, order]


def shift_table():
    root = math.exp(math.log(WRAP_WEIGHT) / LENGTH)
    table = np.zeros((CLASSES, 3, HALF, NODES))
    for c in range(CLASSES):
        angle = 2.0 * np.pi * slot_frequencies(c) / LENGTH
        real = 1.0 - root * np.cos(angle)
        second = real.copy()
        if c == 0:
            second[0] = 1.0 + root
        table[c, 0] = real[:, None]
        table[c, 1] = second[:, None]
        table[c, 2] = (root * np.sin(angle))[:, None]
    table = table.reshape(CLASSES, 3, PARTS, SLOTS, NODES).transpose(0, 2, 1, 3, 4)
    return table.astype(np.float32)


def split_host(matrix):
    high = matrix.astype(jnp.bfloat16)
    low = (matrix - high.astype(np.float64)).astype(jnp.bfloat16)
    return high, low


def split(value):
    high = value.astype(jnp.bfloat16)
    return high, (value - high.astype(jnp.float32)).astype(jnp.bfloat16)


def dot(a, b):
    return jnp.dot(a, b, preferred_element_type=jnp.float32)


BLOCK_GROWTH = [math.exp(math.log(WRAP_WEIGHT) * q / 16.0) for q in range(16)]


def real_dft16(s):
    u = [s[r] + s[r + 8] for r in range(8)]
    w = [s[r] - s[r + 8] for r in range(8)]
    p = [u[r] + u[r + 4] for r in range(4)]
    t = [u[r] - u[r + 4] for r in range(4)]
    out = [None] * 8
    a, b = p[0] + p[2], p[1] + p[3]
    out[0] = (a + b, a - b)
    out[4] = (p[0] - p[2], p[3] - p[1])
    minus, plus = ROOT2 * (t[1] - t[3]), ROOT2 * (t[1] + t[3])
    out[2] = (t[0] + minus, -t[2] - plus)
    out[6] = (t[0] - minus, t[2] - plus)
    lower = [w[r] - w[8 - r] for r in (1, 2, 3)]
    upper = [w[r] + w[8 - r] for r in (1, 2, 3)]
    for c in (1, 3, 5, 7):
        real = w[0]
        imag = -w[4] if c % 4 == 1 else w[4]
        for r in (1, 2, 3):
            real = real + math.cos(math.pi * c * r / 8) * lower[r - 1]
            imag = imag - math.sin(math.pi * c * r / 8) * upper[r - 1]
        out[c] = (real, imag)
    return out


def real_idft16(v):
    (v0, v8), (r2, i2), (r4, i4), (r6, i6) = v[0], v[2], v[4], v[6]
    a, b = v0 + v8, v0 - v8
    ee = [a + r4, b - i4, a - r4, b + i4]
    x, y = r2 - r6, i2 + i6
    eo = [r2 + r6, ROOT2 * (x - y), i6 - i2, -ROOT2 * (x + y)]
    even = [ee[q] + eo[q] for q in range(4)] + [ee[q] - eo[q] for q in range(4)]
    odd = [None] * 8
    odd[0] = (v[1][0] + v[3][0]) + (v[5][0] + v[7][0])
    odd[4] = (v[3][1] - v[1][1]) + (v[7][1] - v[5][1])
    for q in (1, 2, 3):
        real = sum(math.cos(math.pi * c * q / 8) * v[c][0] for c in (1, 3, 5, 7))
        imag = sum(math.sin(math.pi * c * q / 8) * v[c][1] for c in (1, 3, 5, 7))
        odd[q] = real - imag
        odd[8 - q] = -real - imag
    return [even[q] + odd[q] for q in range(8)] + [even[q] - odd[q] for q in range(8)]


CHUNK = 16


def forward_kernel(x_ref, high_ref, low_ref, out_ref, z_ref):
    @pl.loop(0, HALF // CHUNK)
    def _(step):
        row = pl.multiple_of(step * CHUNK, CHUNK)
        series = [
            x_ref[q // 2, pl.ds(q % 2 * HALF + row, CHUNK), :] * BLOCK_GROWTH[q] for q in range(16)
        ]
        for c, pair in enumerate(real_dft16(series)):
            for part in range(2):
                high, low = split(pair[part])
                z_ref[c, pl.ds(part * HALF + row, CHUNK), :NODES] = high
                z_ref[c, pl.ds(part * HALF + row, CHUNK), NODES:] = low

    for c in range(CLASSES):
        both = dot(high_ref[c], z_ref[c])
        out_ref[c] = both[:, :NODES] + both[:, NODES:] + dot(low_ref[c], z_ref[c, :, :NODES])


def inverse_kernel(y_ref, high_ref, low_ref, out_ref, v_ref):
    for c in range(CLASSES):
        high, low = split(y_ref[c])
        both = dot(high_ref[c], jnp.concatenate([high, low], 1))
        v_ref[c] = both[:, :NODES] + both[:, NODES:] + dot(low_ref[c], high)

    @pl.loop(0, HALF // CHUNK)
    def _(step):
        row = pl.multiple_of(step * CHUNK, CHUNK)
        pairs = [
            (v_ref[c, pl.ds(row, CHUNK), :], v_ref[c, pl.ds(HALF + row, CHUNK), :])
            for c in range(CLASSES)
        ]
        for q, value in enumerate(real_idft16(pairs)):
            out_ref[q // 2, pl.ds(q % 2 * HALF + row, CHUNK), :] = value * (1.0 / BLOCK_GROWTH[q])


def weights_kernel(core_ref, blocks_ref, near_ref, far_ref):
    core = core_ref[0]
    for e in range(PLANE):
        for place, s in enumerate(OWN_SLOTS + (2 - core,)):
            high, low = split(blocks_ref[e, s].T)
            near_ref[e, place * NODES : (place + 1) * NODES, :NODES] = high
            near_ref[e, place * NODES : (place + 1) * NODES, NODES:] = low
        high, low = split(blocks_ref[e, 1 + core].T)
        far_ref[e, :, :NODES] = high
        far_ref[e, :, NODES:] = low


def solved(shift_ref, part, shift):
    first = shift_ref[part, 0] + shift
    second = shift_ref[part, 1] + shift
    imaginary = shift_ref[part, 2]
    scale = 1.0 / (first * second + imaginary * imaginary)
    a, b, c = second * scale, imaginary * scale, first * scale

    def apply(value):
        real, imag = value[:SLOTS], value[SLOTS:]
        return jnp.concatenate([a * real + b * imag, c * imag - b * real], 0)

    return apply


def rows_of(part):
    return slice(part * ROWS, (part + 1) * ROWS)


def first_kernel(part, rates_ref, spec_ref, shift_ref, out_ref):
    apply = solved(shift_ref, part, STEP_SCALE * rates_ref[0])
    for e in range(PLANE):
        out_ref[e] = apply(spec_ref[e, rows_of(part)])


def folded(product):
    return (product[:ROWS, :NODES] + product[:ROWS, NODES:]) + (
        product[ROWS:, :NODES] + product[ROWS:, NODES:]
    )


def near_kernel(
    part, sweep, rates_ref, core_ref, nb_ref, y_ref, pair_ref, spec_ref, weights_ref, out_ref, split_ref
):
    core = core_ref[0]
    keep = STEP_SCALE * rates_ref[sweep] - STEP_SCALE * DIAG_WEIGHT
    for place, ref in enumerate((y_ref, pair_ref)):
        for e in range(PLANE):
            high, low = split(ref[e])
            split_ref[place * PLANE + e, :ROWS] = high
            split_ref[place * PLANE + e, ROWS:] = low
    for e in range(PLANE):
        picked = [nb_ref[e, s] % PLANE for s in OWN_SLOTS] + [PLANE + nb_ref[e, 2 - core] % PLANE]
        product = dot(jnp.concatenate([split_ref[i] for i in picked], 1), weights_ref[e])
        out_ref[e] = (
            spec_ref[e, rows_of(part)]
            + keep * y_ref[e]
            - (STEP_SCALE * BLOCK_WEIGHT) * folded(product)
        )


def far_kernel(part, sweep, rates_ref, core_ref, nb_ref, base_ref, far_ref, shift_ref, weights_ref, *rest):
    core = core_ref[0]
    apply = solved(shift_ref, part, STEP_SCALE * rates_ref[sweep])
    out_ref = rest[-1]
    for e in range(PLANE):
        product = dot(
            jnp.concatenate(split(far_ref[nb_ref[e, 1 + core] % PLANE]), 0), weights_ref[e]
        )
        result = apply(base_ref[e] - (STEP_SCALE * BLOCK_WEIGHT) * folded(product))
        if len(rest) == 1:
            out_ref[e] = result
        else:
            for other in range(PARTS - 1):
                out_ref[e, rows_of(other)] = rest[other][e]
            out_ref[e, rows_of(part)] = result


def whole(count):
    return [pl.BlockSpec(memory_space=pltpu.VMEM)] * count


def scalars(count):
    return [pl.BlockSpec(memory_space=pltpu.SMEM)] * count


def call(kernel, outs, specs, flops, moved, scratch=()):
    return pl.pallas_call(
        kernel,
        out_shape=outs,
        in_specs=specs,
        out_specs=jax.tree.map(lambda _: pl.BlockSpec(memory_space=pltpu.VMEM), outs),
        scratch_shapes=scratch,
        compiler_params=pltpu.CompilerParams(vmem_limit_bytes=VMEM_LIMIT),
        cost_estimate=pl.CostEstimate(flops=flops, bytes_accessed=moved, transcendentals=0),
    )


STEPS = jax.ShapeDtypeStruct((PLANE, 2 * HALF, NODES), jnp.float32)
STATE = jax.ShapeDtypeStruct((PLANE, ROWS, NODES), jnp.float32)
MIB = 1 << 20


def per_device(right_side, blocks, neighbors, shift_rates):
    forward, inverse = transform_tables()
    forward_high, forward_low = (jnp.asarray(part) for part in split_host(forward))
    inverse_high, inverse_low = (jnp.asarray(part) for part in split_host(inverse))
    shifts = lax.dynamic_index_in_dim(
        jnp.asarray(shift_table()), lax.axis_index("tm"), 0, keepdims=False
    )
    core = (lax.axis_index("space") % 2).astype(jnp.int32).reshape(1)
    ring = lax.axis_size("space")
    on_chip = [(i, i ^ 1) for i in range(ring)]
    off_chip = [(i, (i + 1 if i % 2 else i - 1) % ring) for i in range(ring)]

    def exchange(value):
        return lax.all_to_all(value, "tm", 0, 0, tiled=True)

    near_weights, far_weights = call(
        weights_kernel,
        (
            jax.ShapeDtypeStruct((PLANE, 6 * NODES, 2 * NODES), jnp.bfloat16),
            jax.ShapeDtypeStruct((PLANE, NODES, 2 * NODES), jnp.bfloat16),
        ),
        scalars(1) + whole(1),
        0,
        8 * MIB,
    )(core, blocks)
    steps = exchange(right_side)
    steps, near_weights, far_weights, shifts = lax.optimization_barrier(
        (steps, near_weights, far_weights, shifts)
    )
    spectrum = call(
        forward_kernel,
        STEPS,
        whole(3),
        10**9,
        4 * MIB,
        [pltpu.VMEM((CLASSES, 256, 256), jnp.bfloat16)],
    )(steps, forward_high, forward_low)
    spectrum = exchange(spectrum)
    states = [
        call(functools.partial(first_kernel, part), STATE, scalars(1) + whole(2), 0, 2 * MIB // PARTS)(
            shift_rates, spectrum, shifts
        )
        for part in range(PARTS)
    ]
    for sweep in range(1, SWEEPS):
        for part in range(PARTS):
            state = states[part]
            pair = lax.ppermute(state, "space", on_chip)
            far = lax.ppermute(state, "space", off_chip)
            base = call(
                functools.partial(near_kernel, part, sweep),
                STATE,
                scalars(3) + whole(4),
                2 * 10**9 // PARTS,
                5 * MIB // PARTS,
                [pltpu.VMEM((2 * PLANE, 2 * ROWS, NODES), jnp.bfloat16)],
            )(shift_rates, core, neighbors, state, pair, spectrum, near_weights)
            last = sweep == SWEEPS - 1 and part == PARTS - 1
            others = states[: PARTS - 1] if last else []
            states[part] = call(
                functools.partial(far_kernel, part, sweep),
                STEPS if last else STATE,
                scalars(3) + whole(4 + len(others)),
                10**9 // PARTS,
                3 * MIB // PARTS,
            )(shift_rates, core, neighbors, base, far, shifts, far_weights, *others)
    steps = call(
        inverse_kernel,
        STEPS,
        whole(3),
        10**9,
        4 * MIB,
        [pltpu.VMEM((CLASSES, 256, 128), jnp.float32)],
    )(exchange(states[-1]), inverse_high, inverse_low)
    return exchange(steps)


def solution(mesh):
    return jax.shard_map(
        per_device,
        mesh=mesh,
        in_specs=(P("space", "tm", None), P("space", None, None, None), P("space", None), P()),
        out_specs=P("space", "tm", None),
        check_vma=False,
    )
```

```python
import functools
import math

import jax
import jax.numpy as jnp
import numpy as np
from jax import lax
from jax.experimental import pallas as pl
from jax.experimental.pallas import tpu as pltpu
from jax.sharding import PartitionSpec as P

SWEEPS = 4
LENGTH = 2048
CLASSES = 8
HALF = 128
PARTS = 2
SLOTS = HALF // PARTS
ROWS = 2 * SLOTS
NODES = 128
PLANE = 8
WRAP_WEIGHT = 0.01
DIAG_WEIGHT = 6.0
BLOCK_WEIGHT = 3.0
STEP_SCALE = 0.1
OWN_SLOTS = (0, 3, 4, 5, 6)
ROOT2 = math.sqrt(0.5)
VMEM_LIMIT = 16 * 1024 * 1024


def slot_frequencies(c):
    j = np.arange(HALF)
    return 8 * j if c == 0 else c + 16 * j


def transform_tables():
    m = np.arange(HALF)
    log_g = math.log(WRAP_WEIGHT) / LENGTH
    forward = np.zeros((CLASSES, 256, 256))
    inverse = np.zeros((CLASSES, 256, 256))
    for c in range(CLASSES):
        k = slot_frequencies(c)
        angle = 2.0 * np.pi * ((k[:, None] * m[None, :]) % LENGTH) / LENGTH
        cos, sin = np.cos(angle), np.sin(angle)
        if c:
            forward[c] = np.block([[cos, sin], [-sin, cos]])
            inverse[c] = np.block([[cos.T, -sin.T], [sin.T, cos.T]]) * (2.0 / LENGTH)
        else:
            even = (np.arange(HALF) % 2 == 0)[:, None]
            sign = np.where(m % 2 == 0, 1.0, -1.0)
            cos_even, cos_odd = cos * even, cos * ~even
            sin_even, sin_odd = sin * even, sin * ~even
            forward[c] = np.block([[cos_even, cos_odd], [-sin_even, -sin_odd]])
            forward[c, HALF, :HALF] = sign
            back = np.block([[cos_even.T, -sin_even.T], [cos_odd.T, -sin_odd.T]]) * (2.0 / LENGTH)
            back[:HALF, 0] = 1.0 / LENGTH
            back[:HALF, HALF] = sign / LENGTH
            inverse[c] = back
    growth = np.exp(log_g * m)
    forward *= np.tile(growth, 2)[None, None, :]
    inverse /= np.tile(growth, 2)[None, :, None]
    order = np.arange(256).reshape(2, PARTS, SLOTS).transpose(1, 0, 2).reshape(256)
    return forward[:, order], inverse[:, :, order]


def shift_table():
    root = math.exp(math.log(WRAP_WEIGHT) / LENGTH)
    table = np.zeros((3, HALF, NODES))
    for c in range(CLASSES):
        angle = 2.0 * np.pi * slot_frequencies(c) / LENGTH
        real = 1.0 - root * np.cos(angle)
        second = real.copy()
        if c == 0:
            second[0] = 1.0 + root
        table[0, :, c] = real
        table[1, :, c] = second
        table[2, :, c] = root * np.sin(angle)
    return table.reshape(3, PARTS, SLOTS, NODES).transpose(1, 0, 2, 3).astype(np.float32)


def split_host(matrix):
    high = matrix.astype(jnp.bfloat16)
    low = (matrix - high.astype(np.float64)).astype(jnp.bfloat16)
    return high, low


def split(value):
    high = value.astype(jnp.bfloat16)
    return high, (value - high.astype(jnp.float32)).astype(jnp.bfloat16)


def dot(a, b):
    return jnp.dot(a, b, preferred_element_type=jnp.float32)


BLOCK_GROWTH = [math.exp(math.log(WRAP_WEIGHT) * q / 16.0) for q in range(16)]


def real_dft16(s):
    u = [s[r] + s[r + 8] for r in range(8)]
    w = [s[r] - s[r + 8] for r in range(8)]
    p = [u[r] + u[r + 4] for r in range(4)]
    t = [u[r] - u[r + 4] for r in range(4)]
    out = [None] * 8
    a, b = p[0] + p[2], p[1] + p[3]
    out[0] = (a + b, a - b)
    out[4] = (p[0] - p[2], p[3] - p[1])
    minus, plus = ROOT2 * (t[1] - t[3]), ROOT2 * (t[1] + t[3])
    out[2] = (t[0] + minus, -t[2] - plus)
    out[6] = (t[0] - minus, t[2] - plus)
    lower = [w[r] - w[8 - r] for r in (1, 2, 3)]
    upper = [w[r] + w[8 - r] for r in (1, 2, 3)]
    for c in (1, 3, 5, 7):
        real = w[0]
        imag = -w[4] if c % 4 == 1 else w[4]
        for r in (1, 2, 3):
            real = real + math.cos(math.pi * c * r / 8) * lower[r - 1]
            imag = imag - math.sin(math.pi * c * r / 8) * upper[r - 1]
        out[c] = (real, imag)
    return out


def real_idft16(v):
    (v0, v8), (r2, i2), (r4, i4), (r6, i6) = v[0], v[2], v[4], v[6]
    a, b = v0 + v8, v0 - v8
    ee = [a + r4, b - i4, a - r4, b + i4]
    x, y = r2 - r6, i2 + i6
    eo = [r2 + r6, ROOT2 * (x - y), i6 - i2, -ROOT2 * (x + y)]
    even = [ee[q] + eo[q] for q in range(4)] + [ee[q] - eo[q] for q in range(4)]
    odd = [None] * 8
    odd[0] = (v[1][0] + v[3][0]) + (v[5][0] + v[7][0])
    odd[4] = (v[3][1] - v[1][1]) + (v[7][1] - v[5][1])
    for q in (1, 2, 3):
        real = sum(math.cos(math.pi * c * q / 8) * v[c][0] for c in (1, 3, 5, 7))
        imag = sum(math.sin(math.pi * c * q / 8) * v[c][1] for c in (1, 3, 5, 7))
        odd[q] = real - imag
        odd[8 - q] = -real - imag
    return [even[q] + odd[q] for q in range(8)] + [even[q] - odd[q] for q in range(8)]


CHUNK = 16


def steps_at(q, row):
    return q // 2, pl.ds(q % 2 * HALF + row, CHUNK), slice(None)


def table_product(high, low, value):
    value_high, value_low = split(value)
    both = dot(high, jnp.concatenate([value_high, value_low], 1))
    return both[:, :NODES] + both[:, NODES:] + dot(low, value_high)


def forward_kernel(x_ref, out_ref):
    @pl.loop(0, HALF // CHUNK)
    def _(step):
        row = pl.multiple_of(step * CHUNK, CHUNK)
        series = [x_ref[steps_at(q, row)] * BLOCK_GROWTH[q] for q in range(16)]
        for c, (real, imag) in enumerate(real_dft16(series)):
            out_ref[c, pl.ds(row, CHUNK), :] = real
            out_ref[c, pl.ds(HALF + row, CHUNK), :] = imag


def inverse_kernel(y_ref, high_ref, low_ref, out_ref, v_ref):
    for c in range(CLASSES):
        v_ref[c] = table_product(high_ref[c], low_ref[c], y_ref[c])

    @pl.loop(0, HALF // CHUNK)
    def _(step):
        row = pl.multiple_of(step * CHUNK, CHUNK)
        pairs = [
            (v_ref[c, pl.ds(row, CHUNK), :], v_ref[c, pl.ds(HALF + row, CHUNK), :])
            for c in range(CLASSES)
        ]
        for q, value in enumerate(real_idft16(pairs)):
            out_ref[steps_at(q, row)] = value * (1.0 / BLOCK_GROWTH[q])


def weights_kernel(here_ref, blocks_ref, _, near_ref, far_ref):
    core = here_ref[0] % 2
    for e in range(PLANE):
        for place, s in enumerate(OWN_SLOTS + (2 - core,)):
            high, low = split(blocks_ref[e, s].T)
            near_ref[e, place * NODES : (place + 1) * NODES, :NODES] = high
            near_ref[e, place * NODES : (place + 1) * NODES, NODES:] = low
        high, low = split(blocks_ref[e, 1 + core].T)
        far_ref[e, :, :NODES] = high
        far_ref[e, :, NODES:] = low


def solved(here_ref, shift_ref, part, shift):
    mine = lax.broadcasted_iota(jnp.int32, (SLOTS, NODES), 1) == here_ref[0] // 2
    real, second, imaginary = (
        jnp.sum(jnp.where(mine, shift_ref[part, i], 0.0), 1, keepdims=True) for i in range(3)
    )
    first = real + shift
    second = second + shift
    scale = 1.0 / (first * second + imaginary * imaginary)
    a, b, c = (
        jnp.broadcast_to(factor * scale, (SLOTS, NODES)) for factor in (second, imaginary, first)
    )

    def apply(value):
        real, imag = value[:SLOTS], value[SLOTS:]
        return jnp.concatenate([a * real + b * imag, c * imag - b * real], 0)

    return apply


def rows_of(part):
    return slice(part * ROWS, (part + 1) * ROWS)


def first_kernel(part, rates_ref, here_ref, series_ref, high_ref, low_ref, shift_ref, spec_ref, out_ref):
    apply = solved(here_ref, shift_ref, part, STEP_SCALE * rates_ref[0])
    mine = here_ref[0] // 2
    high, low = high_ref[mine, rows_of(part)], low_ref[mine, rows_of(part)]
    for e in range(PLANE):
        spec = table_product(high, low, series_ref[e])
        spec_ref[e] = spec
        out_ref[e] = apply(spec)


def folded(product):
    return (product[:ROWS, :NODES] + product[:ROWS, NODES:]) + (
        product[ROWS:, :NODES] + product[ROWS:, NODES:]
    )


def near_kernel(
    part, sweep, rates_ref, here_ref, nb_ref, y_ref, pair_ref, spec_ref, weights_ref, out_ref, split_ref
):
    core = here_ref[0] % 2
    keep = STEP_SCALE * rates_ref[sweep] - STEP_SCALE * DIAG_WEIGHT
    for place, ref in enumerate((y_ref, pair_ref)):
        for e in range(PLANE):
            high, low = split(ref[e])
            split_ref[place * PLANE + e, :ROWS] = high
            split_ref[place * PLANE + e, ROWS:] = low
    for e in range(PLANE):
        picked = [nb_ref[e, s] % PLANE for s in OWN_SLOTS] + [PLANE + nb_ref[e, 2 - core] % PLANE]
        product = dot(jnp.concatenate([split_ref[i] for i in picked], 1), weights_ref[e])
        out_ref[e] = (
            spec_ref[e]
            + keep * y_ref[e]
            - (STEP_SCALE * BLOCK_WEIGHT) * folded(product)
        )


def far_kernel(part, sweep, rates_ref, here_ref, nb_ref, base_ref, far_ref, shift_ref, weights_ref, *rest):
    core = here_ref[0] % 2
    apply = solved(here_ref, shift_ref, part, STEP_SCALE * rates_ref[sweep])
    out_ref = rest[-1]
    for e in range(PLANE):
        product = dot(
            jnp.concatenate(split(far_ref[nb_ref[e, 1 + core] % PLANE]), 0), weights_ref[e]
        )
        result = apply(base_ref[e] - (STEP_SCALE * BLOCK_WEIGHT) * folded(product))
        if len(rest) == 1:
            out_ref[e] = result
        else:
            for other in range(PARTS - 1):
                out_ref[e, rows_of(other)] = rest[other][e]
            out_ref[e, rows_of(part)] = result


def whole(count):
    return [pl.BlockSpec(memory_space=pltpu.VMEM)] * count


def scalars(count):
    return [pl.BlockSpec(memory_space=pltpu.SMEM)] * count


def call(kernel, outs, specs, flops, moved, scratch=()):
    return pl.pallas_call(
        kernel,
        out_shape=outs,
        in_specs=specs,
        out_specs=jax.tree.map(lambda _: pl.BlockSpec(memory_space=pltpu.VMEM), outs),
        scratch_shapes=scratch,
        compiler_params=pltpu.CompilerParams(vmem_limit_bytes=VMEM_LIMIT),
        cost_estimate=pl.CostEstimate(flops=flops, bytes_accessed=moved, transcendentals=0),
    )


STEPS = jax.ShapeDtypeStruct((PLANE, 2 * HALF, NODES), jnp.float32)
STATE = jax.ShapeDtypeStruct((PLANE, ROWS, NODES), jnp.float32)
MIB = 1 << 20


def per_device(right_side, blocks, neighbors, shift_rates):
    forward, inverse = transform_tables()
    forward_high, forward_low = (jnp.asarray(part) for part in split_host(forward))
    inverse_high, inverse_low = (jnp.asarray(part) for part in split_host(inverse))
    shifts = jnp.asarray(shift_table())
    here = (lax.axis_index("tm") * 2 + (lax.axis_index("space") & 1)).astype(jnp.int32).reshape(1)
    right_side, here = lax.optimization_barrier((right_side, here))
    ring = lax.axis_size("space")
    on_chip = [(i, i ^ 1) for i in range(ring)]
    off_chip = [(i, (i + 1 if i % 2 else i - 1) % ring) for i in range(ring)]

    def exchange(value):
        return lax.all_to_all(value, "tm", 0, 0, tiled=True)

    series = exchange(call(forward_kernel, STEPS, whole(1), 0, 2 * MIB)(exchange(right_side)))
    spectrum, states = zip(
        *(
            call(
                functools.partial(first_kernel, part),
                (STATE, STATE),
                scalars(2) + whole(4),
                10**9 // PARTS,
                4 * MIB // PARTS,
            )(shift_rates, here, series, forward_high, forward_low, shifts)
            for part in range(PARTS)
        )
    )
    states = list(states)
    near_weights, far_weights = call(
        weights_kernel,
        (
            jax.ShapeDtypeStruct((PLANE, 6 * NODES, 2 * NODES), jnp.bfloat16),
            jax.ShapeDtypeStruct((PLANE, NODES, 2 * NODES), jnp.bfloat16),
        ),
        scalars(1) + whole(1) + [pl.BlockSpec(memory_space=pl.ANY)],
        0,
        8 * MIB,
    )(here, blocks, states[0])
    for sweep in range(1, SWEEPS):
        for part in range(PARTS):
            state = states[part]
            pair = lax.ppermute(state, "space", on_chip)
            far = lax.ppermute(state, "space", off_chip)
            base = call(
                functools.partial(near_kernel, part, sweep),
                STATE,
                scalars(3) + whole(4),
                2 * 10**9 // PARTS,
                5 * MIB // PARTS,
                [pltpu.VMEM((2 * PLANE, 2 * ROWS, NODES), jnp.bfloat16)],
            )(shift_rates, here, neighbors, state, pair, spectrum[part], near_weights)
            last = sweep == SWEEPS - 1 and part == PARTS - 1
            others = states[: PARTS - 1] if last else []
            states[part] = call(
                functools.partial(far_kernel, part, sweep),
                STEPS if last else STATE,
                scalars(3) + whole(4 + len(others)),
                10**9 // PARTS,
                3 * MIB // PARTS,
            )(shift_rates, here, neighbors, base, far, shifts, far_weights, *others)
    steps = call(
        inverse_kernel,
        STEPS,
        whole(3),
        10**9,
        4 * MIB,
        [pltpu.VMEM((CLASSES, 256, NODES), jnp.float32)],
    )(exchange(states[-1]), inverse_high, inverse_low)
    return exchange(steps)


def solution(mesh):
    return jax.shard_map(
        per_device,
        mesh=mesh,
        in_specs=(P("space", "tm", None), P("space", None, None, None), P("space", None), P()),
        out_specs=P("space", "tm", None),
        check_vma=False,
    )
```

```python
import functools
import math

import jax
import jax.numpy as jnp
import numpy as np
from jax import lax
from jax.experimental import pallas as pl
from jax.experimental.pallas import tpu as pltpu
from jax.sharding import PartitionSpec as P

SWEEPS = 4
LENGTH = 2048
CLASSES = 8
HALF = 128
PARTS = 2
SLOTS = HALF // PARTS
ROWS = 2 * SLOTS
NODES = 128
PLANE = 8
WRAP_WEIGHT = 0.01
DIAG_WEIGHT = 6.0
BLOCK_WEIGHT = 3.0
STEP_SCALE = 0.1
OWN_SLOTS = (0, 3, 4, 5, 6)
ROOT2 = math.sqrt(0.5)
VMEM_LIMIT = 16 * 1024 * 1024


def slot_frequencies(c):
    j = np.arange(HALF)
    return 8 * j if c == 0 else c + 16 * j


def transform_tables():
    m = np.arange(HALF)
    log_g = math.log(WRAP_WEIGHT) / LENGTH
    forward = np.zeros((CLASSES, 256, 256))
    inverse = np.zeros((CLASSES, 256, 256))
    for c in range(CLASSES):
        k = slot_frequencies(c)
        angle = 2.0 * np.pi * ((k[:, None] * m[None, :]) % LENGTH) / LENGTH
        cos, sin = np.cos(angle), np.sin(angle)
        if c:
            forward[c] = np.block([[cos, sin], [-sin, cos]])
            inverse[c] = np.block([[cos.T, -sin.T], [sin.T, cos.T]]) * (2.0 / LENGTH)
        else:
            even = (np.arange(HALF) % 2 == 0)[:, None]
            sign = np.where(m % 2 == 0, 1.0, -1.0)
            cos_even, cos_odd = cos * even, cos * ~even
            sin_even, sin_odd = sin * even, sin * ~even
            forward[c] = np.block([[cos_even, cos_odd], [-sin_even, -sin_odd]])
            forward[c, HALF, :HALF] = sign
            back = np.block([[cos_even.T, -sin_even.T], [cos_odd.T, -sin_odd.T]]) * (2.0 / LENGTH)
            back[:HALF, 0] = 1.0 / LENGTH
            back[:HALF, HALF] = sign / LENGTH
            inverse[c] = back
    growth = np.exp(log_g * m)
    forward *= np.tile(growth, 2)[None, None, :]
    inverse /= np.tile(growth, 2)[None, :, None]
    order = np.arange(256).reshape(2, PARTS, SLOTS).transpose(1, 0, 2).reshape(256)
    return forward[:, order], inverse[:, :, order]


def shift_table():
    root = math.exp(math.log(WRAP_WEIGHT) / LENGTH)
    table = np.zeros((3, HALF, NODES))
    for c in range(CLASSES):
        angle = 2.0 * np.pi * slot_frequencies(c) / LENGTH
        real = 1.0 - root * np.cos(angle)
        second = real.copy()
        if c == 0:
            second[0] = 1.0 + root
        table[0, :, c] = real
        table[1, :, c] = second
        table[2, :, c] = root * np.sin(angle)
    return table.reshape(3, PARTS, SLOTS, NODES).transpose(1, 0, 2, 3).astype(np.float32)


def split_host(matrix):
    high = matrix.astype(jnp.bfloat16)
    low = (matrix - high.astype(np.float64)).astype(jnp.bfloat16)
    return high, low


def split(value):
    high = value.astype(jnp.bfloat16)
    return high, (value - high.astype(jnp.float32)).astype(jnp.bfloat16)


def dot(a, b):
    return jnp.dot(a, b, preferred_element_type=jnp.float32)


BLOCK_GROWTH = [math.exp(math.log(WRAP_WEIGHT) * q / 16.0) for q in range(16)]


def real_dft16(s):
    u = [s[r] + s[r + 8] for r in range(8)]
    w = [s[r] - s[r + 8] for r in range(8)]
    p = [u[r] + u[r + 4] for r in range(4)]
    t = [u[r] - u[r + 4] for r in range(4)]
    out = [None] * 8
    a, b = p[0] + p[2], p[1] + p[3]
    out[0] = (a + b, a - b)
    out[4] = (p[0] - p[2], p[3] - p[1])
    minus, plus = ROOT2 * (t[1] - t[3]), ROOT2 * (t[1] + t[3])
    out[2] = (t[0] + minus, -t[2] - plus)
    out[6] = (t[0] - minus, t[2] - plus)
    lower = [w[r] - w[8 - r] for r in (1, 2, 3)]
    upper = [w[r] + w[8 - r] for r in (1, 2, 3)]
    for c in (1, 3, 5, 7):
        real = w[0]
        imag = -w[4] if c % 4 == 1 else w[4]
        for r in (1, 2, 3):
            real = real + math.cos(math.pi * c * r / 8) * lower[r - 1]
            imag = imag - math.sin(math.pi * c * r / 8) * upper[r - 1]
        out[c] = (real, imag)
    return out


def real_idft16(v):
    (v0, v8), (r2, i2), (r4, i4), (r6, i6) = v[0], v[2], v[4], v[6]
    a, b = v0 + v8, v0 - v8
    ee = [a + r4, b - i4, a - r4, b + i4]
    x, y = r2 - r6, i2 + i6
    eo = [r2 + r6, ROOT2 * (x - y), i6 - i2, -ROOT2 * (x + y)]
    even = [ee[q] + eo[q] for q in range(4)] + [ee[q] - eo[q] for q in range(4)]
    odd = [None] * 8
    odd[0] = (v[1][0] + v[3][0]) + (v[5][0] + v[7][0])
    odd[4] = (v[3][1] - v[1][1]) + (v[7][1] - v[5][1])
    for q in (1, 2, 3):
        real = sum(math.cos(math.pi * c * q / 8) * v[c][0] for c in (1, 3, 5, 7))
        imag = sum(math.sin(math.pi * c * q / 8) * v[c][1] for c in (1, 3, 5, 7))
        odd[q] = real - imag
        odd[8 - q] = -real - imag
    return [even[q] + odd[q] for q in range(8)] + [even[q] - odd[q] for q in range(8)]


CHUNK = 16


def steps_at(q, row):
    return q // 2, pl.ds(q % 2 * HALF + row, CHUNK), slice(None)


def table_product(high, low, value):
    value_high, value_low = split(value)
    both = dot(high, jnp.concatenate([value_high, value_low], 1))
    return both[:, :NODES] + both[:, NODES:] + dot(low, value_high)


def forward_kernel(x_ref, out_ref):
    @pl.loop(0, HALF // CHUNK)
    def _(step):
        row = pl.multiple_of(step * CHUNK, CHUNK)
        series = [x_ref[steps_at(q, row)] * BLOCK_GROWTH[q] for q in range(16)]
        for c, (real, imag) in enumerate(real_dft16(series)):
            out_ref[c, pl.ds(row, CHUNK), :] = real
            out_ref[c, pl.ds(HALF + row, CHUNK), :] = imag


def inverse_kernel(y_ref, high_ref, low_ref, out_ref, v_ref):
    for c in range(CLASSES):
        v_ref[c] = table_product(high_ref[c], low_ref[c], y_ref[c])

    @pl.loop(0, HALF // CHUNK)
    def _(step):
        row = pl.multiple_of(step * CHUNK, CHUNK)
        pairs = [
            (v_ref[c, pl.ds(row, CHUNK), :], v_ref[c, pl.ds(HALF + row, CHUNK), :])
            for c in range(CLASSES)
        ]
        for q, value in enumerate(real_idft16(pairs)):
            out_ref[steps_at(q, row)] = value * (1.0 / BLOCK_GROWTH[q])


def weights_kernel(here_ref, blocks_ref, _, near_ref, far_ref):
    core = here_ref[0] % 2
    for e in range(PLANE):
        for place, s in enumerate(OWN_SLOTS + (2 - core,)):
            high, low = split(blocks_ref[e, s].T)
            near_ref[e, place * NODES : (place + 1) * NODES, :NODES] = high
            near_ref[e, place * NODES : (place + 1) * NODES, NODES:] = low
        high, low = split(blocks_ref[e, 1 + core].T)
        far_ref[e, :, :NODES] = high
        far_ref[e, :, NODES:] = low


def solved(here_ref, shift_ref, part, shift):
    mine = lax.broadcasted_iota(jnp.int32, (SLOTS, NODES), 1) == here_ref[0] // 2
    real, second, imaginary = (
        jnp.sum(jnp.where(mine, shift_ref[part, i], 0.0), 1, keepdims=True) for i in range(3)
    )
    first = real + shift
    second = second + shift
    scale = 1.0 / (first * second + imaginary * imaginary)
    a, b, c = (
        jnp.broadcast_to(factor * scale, (SLOTS, NODES)) for factor in (second, imaginary, first)
    )

    def apply(value):
        real, imag = value[:SLOTS], value[SLOTS:]
        return jnp.concatenate([a * real + b * imag, c * imag - b * real], 0)

    return apply


def rows_of(part):
    return slice(part * ROWS, (part + 1) * ROWS)


def first_kernel(part, rates_ref, here_ref, series_ref, high_ref, low_ref, shift_ref, spec_ref, out_ref):
    apply = solved(here_ref, shift_ref, part, STEP_SCALE * rates_ref[0])
    mine = here_ref[0] // 2
    high, low = high_ref[mine, rows_of(part)], low_ref[mine, rows_of(part)]
    for e in range(PLANE):
        spec = table_product(high, low, series_ref[e])
        spec_ref[e] = spec
        out_ref[e] = apply(spec)


def folded(product):
    return (product[:ROWS, :NODES] + product[:ROWS, NODES:]) + (
        product[ROWS:, :NODES] + product[ROWS:, NODES:]
    )


def near_kernel(
    part, sweep, rates_ref, here_ref, nb_ref, y_ref, pair_ref, spec_ref, weights_ref, out_ref, split_ref
):
    core = here_ref[0] % 2
    keep = STEP_SCALE * rates_ref[sweep] - STEP_SCALE * DIAG_WEIGHT
    for place, ref in enumerate((y_ref, pair_ref)):
        for e in range(PLANE):
            high, low = split(ref[e])
            split_ref[place * PLANE + e, :ROWS] = high
            split_ref[place * PLANE + e, ROWS:] = low
    for e in range(PLANE):
        picked = [nb_ref[e, s] % PLANE for s in OWN_SLOTS] + [PLANE + jnp.where(core == 0, nb_ref[e, 2], nb_ref[e, 1]) % PLANE]
        product = dot(jnp.concatenate([split_ref[i] for i in picked], 1), weights_ref[e])
        out_ref[e] = (
            spec_ref[e]
            + keep * y_ref[e]
            - (STEP_SCALE * BLOCK_WEIGHT) * folded(product)
        )


def far_kernel(part, sweep, rates_ref, here_ref, nb_ref, base_ref, far_ref, shift_ref, weights_ref, *rest):
    core = here_ref[0] % 2
    apply = solved(here_ref, shift_ref, part, STEP_SCALE * rates_ref[sweep])
    out_ref = rest[-1]
    for e in range(PLANE):
        picked = jnp.where(core == 0, nb_ref[e, 1], nb_ref[e, 2]) % PLANE
        product = dot(jnp.concatenate(split(far_ref[picked]), 0), weights_ref[e])
        result = apply(base_ref[e] - (STEP_SCALE * BLOCK_WEIGHT) * folded(product))
        if len(rest) == 1:
            out_ref[e] = result
        else:
            for other in range(PARTS - 1):
                out_ref[e, rows_of(other)] = rest[other][e]
            out_ref[e, rows_of(part)] = result


def whole(count):
    return [pl.BlockSpec(memory_space=pltpu.VMEM)] * count


def call(kernel, outs, specs, flops, moved, scratch=()):
    return pl.pallas_call(
        kernel,
        out_shape=outs,
        in_specs=specs,
        out_specs=jax.tree.map(lambda _: pl.BlockSpec(memory_space=pltpu.VMEM), outs),
        scratch_shapes=scratch,
        compiler_params=pltpu.CompilerParams(vmem_limit_bytes=VMEM_LIMIT),
        cost_estimate=pl.CostEstimate(flops=flops, bytes_accessed=moved, transcendentals=0),
    )


STEPS = jax.ShapeDtypeStruct((PLANE, 2 * HALF, NODES), jnp.float32)
STATE = jax.ShapeDtypeStruct((PLANE, ROWS, NODES), jnp.float32)
MIB = 1 << 20


def per_device(right_side, blocks, neighbors, shift_rates):
    forward, inverse = transform_tables()
    forward_high, forward_low = (jnp.asarray(part) for part in split_host(forward))
    inverse_high, inverse_low = (jnp.asarray(part) for part in split_host(inverse))
    shifts = jnp.asarray(shift_table())
    here = (lax.axis_index("tm") * 2 + (lax.axis_index("space") & 1)).astype(jnp.int32).reshape(1)
    right_side, here = lax.optimization_barrier((right_side, here))
    ring = lax.axis_size("space")
    on_chip = [(i, i ^ 1) for i in range(ring)]
    off_chip = [(i, (i + 1 if i % 2 else i - 1) % ring) for i in range(ring)]

    def exchange(value):
        return lax.all_to_all(value, "tm", 0, 0, tiled=True)

    series = exchange(call(forward_kernel, STEPS, whole(1), 0, 2 * MIB)(exchange(right_side)))
    spectrum, states = zip(
        *(
            call(
                functools.partial(first_kernel, part),
                (STATE, STATE),
                whole(6),
                10**9 // PARTS,
                4 * MIB // PARTS,
            )(shift_rates, here, series, forward_high, forward_low, shifts)
            for part in range(PARTS)
        )
    )
    states = list(states)
    near_weights, far_weights = call(
        weights_kernel,
        (
            jax.ShapeDtypeStruct((PLANE, 6 * NODES, 2 * NODES), jnp.bfloat16),
            jax.ShapeDtypeStruct((PLANE, NODES, 2 * NODES), jnp.bfloat16),
        ),
        whole(2) + [pl.BlockSpec(memory_space=pl.ANY)],
        0,
        8 * MIB,
    )(here, blocks, states[0])
    for sweep in range(1, SWEEPS):
        for part in range(PARTS):
            state = states[part]
            pair = lax.ppermute(state, "space", on_chip)
            far = lax.ppermute(state, "space", off_chip)
            base = call(
                functools.partial(near_kernel, part, sweep),
                STATE,
                whole(7),
                2 * 10**9 // PARTS,
                5 * MIB // PARTS,
                [pltpu.VMEM((2 * PLANE, 2 * ROWS, NODES), jnp.bfloat16)],
            )(shift_rates, here, neighbors, state, pair, spectrum[part], near_weights)
            last = sweep == SWEEPS - 1 and part == PARTS - 1
            others = states[: PARTS - 1] if last else []
            states[part] = call(
                functools.partial(far_kernel, part, sweep),
                STEPS if last else STATE,
                whole(7 + len(others)),
                10**9 // PARTS,
                3 * MIB // PARTS,
            )(shift_rates, here, neighbors, base, far, shifts, far_weights, *others)
    steps = call(
        inverse_kernel,
        STEPS,
        whole(3),
        10**9,
        4 * MIB,
        [pltpu.VMEM((CLASSES, 256, NODES), jnp.float32)],
    )(exchange(states[-1]), inverse_high, inverse_low)
    return exchange(steps)


def solution(mesh):
    return jax.shard_map(
        per_device,
        mesh=mesh,
        in_specs=(P("space", "tm", None), P("space", None, None, None), P("space", None), P()),
        out_specs=P("space", "tm", None),
        check_vma=False,
    )
```

```python
import functools
import math

import jax
import jax.numpy as jnp
import numpy as np
from jax import lax
from jax.experimental import pallas as pl
from jax.experimental.pallas import tpu as pltpu
from jax.sharding import PartitionSpec as P

SWEEPS = 4
LENGTH = 2048
CLASSES = 8
HALF = 128
PARTS = 2
SLOTS = HALF // PARTS
ROWS = 2 * SLOTS
NODES = 128
PLANE = 8
WRAP_WEIGHT = 0.01
DIAG_WEIGHT = 6.0
BLOCK_WEIGHT = 3.0
STEP_SCALE = 0.1
OWN_SLOTS = (0, 3, 4, 5, 6)
ROOT2 = math.sqrt(0.5)
VMEM_LIMIT = 16 * 1024 * 1024


def slot_frequencies(c):
    j = np.arange(HALF)
    return 8 * j if c == 0 else c + 16 * j


def transform_tables():
    m = np.arange(HALF)
    log_g = math.log(WRAP_WEIGHT) / LENGTH
    forward = np.zeros((CLASSES, 256, 256))
    inverse = np.zeros((CLASSES, 256, 256))
    for c in range(CLASSES):
        k = slot_frequencies(c)
        angle = 2.0 * np.pi * ((k[:, None] * m[None, :]) % LENGTH) / LENGTH
        cos, sin = np.cos(angle), np.sin(angle)
        if c:
            forward[c] = np.block([[cos, sin], [-sin, cos]])
            inverse[c] = np.block([[cos.T, -sin.T], [sin.T, cos.T]]) * (2.0 / LENGTH)
        else:
            even = (np.arange(HALF) % 2 == 0)[:, None]
            sign = np.where(m % 2 == 0, 1.0, -1.0)
            cos_even, cos_odd = cos * even, cos * ~even
            sin_even, sin_odd = sin * even, sin * ~even
            forward[c] = np.block([[cos_even, cos_odd], [-sin_even, -sin_odd]])
            forward[c, HALF, :HALF] = sign
            back = np.block([[cos_even.T, -sin_even.T], [cos_odd.T, -sin_odd.T]]) * (2.0 / LENGTH)
            back[:HALF, 0] = 1.0 / LENGTH
            back[:HALF, HALF] = sign / LENGTH
            inverse[c] = back
    growth = np.exp(log_g * m)
    forward *= np.tile(growth, 2)[None, None, :]
    inverse /= np.tile(growth, 2)[None, :, None]
    order = np.arange(256).reshape(2, PARTS, SLOTS).transpose(1, 0, 2).reshape(256)
    return forward[:, order], inverse[:, :, order]


def shift_table():
    root = math.exp(math.log(WRAP_WEIGHT) / LENGTH)
    table = np.zeros((3, HALF, NODES))
    for c in range(CLASSES):
        angle = 2.0 * np.pi * slot_frequencies(c) / LENGTH
        real = 1.0 - root * np.cos(angle)
        second = real.copy()
        if c == 0:
            second[0] = 1.0 + root
        table[0, :, c] = real
        table[1, :, c] = second
        table[2, :, c] = root * np.sin(angle)
    return table.reshape(3, PARTS, SLOTS, NODES).transpose(1, 0, 2, 3).astype(np.float32)


def split_host(matrix):
    high = matrix.astype(jnp.bfloat16)
    low = (matrix - high.astype(np.float64)).astype(jnp.bfloat16)
    return high, low


def split(value):
    high = value.astype(jnp.bfloat16)
    return high, (value - high.astype(jnp.float32)).astype(jnp.bfloat16)


def dot(a, b):
    return jnp.dot(a, b, preferred_element_type=jnp.float32)


BLOCK_GROWTH = [math.exp(math.log(WRAP_WEIGHT) * q / 16.0) for q in range(16)]


def real_dft16(s):
    u = [s[r] + s[r + 8] for r in range(8)]
    w = [s[r] - s[r + 8] for r in range(8)]
    p = [u[r] + u[r + 4] for r in range(4)]
    t = [u[r] - u[r + 4] for r in range(4)]
    out = [None] * 8
    a, b = p[0] + p[2], p[1] + p[3]
    out[0] = (a + b, a - b)
    out[4] = (p[0] - p[2], p[3] - p[1])
    minus, plus = ROOT2 * (t[1] - t[3]), ROOT2 * (t[1] + t[3])
    out[2] = (t[0] + minus, -t[2] - plus)
    out[6] = (t[0] - minus, t[2] - plus)
    lower = [w[r] - w[8 - r] for r in (1, 2, 3)]
    upper = [w[r] + w[8 - r] for r in (1, 2, 3)]
    for c in (1, 3, 5, 7):
        real = w[0]
        imag = -w[4] if c % 4 == 1 else w[4]
        for r in (1, 2, 3):
            real = real + math.cos(math.pi * c * r / 8) * lower[r - 1]
            imag = imag - math.sin(math.pi * c * r / 8) * upper[r - 1]
        out[c] = (real, imag)
    return out


def real_idft16(v):
    (v0, v8), (r2, i2), (r4, i4), (r6, i6) = v[0], v[2], v[4], v[6]
    a, b = v0 + v8, v0 - v8
    ee = [a + r4, b - i4, a - r4, b + i4]
    x, y = r2 - r6, i2 + i6
    eo = [r2 + r6, ROOT2 * (x - y), i6 - i2, -ROOT2 * (x + y)]
    even = [ee[q] + eo[q] for q in range(4)] + [ee[q] - eo[q] for q in range(4)]
    odd = [None] * 8
    odd[0] = (v[1][0] + v[3][0]) + (v[5][0] + v[7][0])
    odd[4] = (v[3][1] - v[1][1]) + (v[7][1] - v[5][1])
    for q in (1, 2, 3):
        real = sum(math.cos(math.pi * c * q / 8) * v[c][0] for c in (1, 3, 5, 7))
        imag = sum(math.sin(math.pi * c * q / 8) * v[c][1] for c in (1, 3, 5, 7))
        odd[q] = real - imag
        odd[8 - q] = -real - imag
    return [even[q] + odd[q] for q in range(8)] + [even[q] - odd[q] for q in range(8)]


CHUNK = 16
ORDERS = ((0, 4, 2, 6, 3, 7, 1, 5), (5, 1, 7, 3, 6, 2, 4, 0))


def places_of(here_ref):
    return [
        jnp.where(here_ref[0] % 2 == 0, ORDERS[0].index(p), ORDERS[1].index(p)) for p in range(8)
    ]


def steps_at(places, q, row):
    return places[q // 2], pl.ds(q % 2 * HALF + row, CHUNK), slice(None)


def table_product(high, low, value):
    value_high, value_low = split(value)
    both = dot(high, jnp.concatenate([value_high, value_low], 1))
    return both[:, :NODES] + both[:, NODES:] + dot(low, value_high)


def forward_kernel(here_ref, x_ref, out_ref):
    places = places_of(here_ref)

    @pl.loop(0, HALF // CHUNK)
    def _(step):
        row = pl.multiple_of(step * CHUNK, CHUNK)
        series = [x_ref[steps_at(places, q, row)] * BLOCK_GROWTH[q] for q in range(16)]
        for c, (real, imag) in enumerate(real_dft16(series)):
            out_ref[places[c], pl.ds(row, CHUNK), :] = real
            out_ref[places[c], pl.ds(HALF + row, CHUNK), :] = imag


def inverse_kernel(here_ref, y_ref, high_ref, low_ref, out_ref, v_ref):
    places = places_of(here_ref)
    for c in range(CLASSES):
        v_ref[c] = table_product(high_ref[c], low_ref[c], y_ref[places[c]])

    @pl.loop(0, HALF // CHUNK)
    def _(step):
        row = pl.multiple_of(step * CHUNK, CHUNK)
        pairs = [
            (v_ref[c, pl.ds(row, CHUNK), :], v_ref[c, pl.ds(HALF + row, CHUNK), :])
            for c in range(CLASSES)
        ]
        for q, value in enumerate(real_idft16(pairs)):
            out_ref[steps_at(places, q, row)] = value * (1.0 / BLOCK_GROWTH[q])


def weights_kernel(here_ref, blocks_ref, _, near_ref, far_ref):
    core = here_ref[0] % 2
    for e in range(PLANE):
        for place, s in enumerate(OWN_SLOTS + (2 - core,)):
            high, low = split(blocks_ref[e, s].T)
            near_ref[e, place * NODES : (place + 1) * NODES, :NODES] = high
            near_ref[e, place * NODES : (place + 1) * NODES, NODES:] = low
        high, low = split(blocks_ref[e, 1 + core].T)
        far_ref[e, :, :NODES] = high
        far_ref[e, :, NODES:] = low


def solved(here_ref, shift_ref, part, shift):
    mine = lax.broadcasted_iota(jnp.int32, (SLOTS, NODES), 1) == here_ref[0] // 2
    real, second, imaginary = (
        jnp.sum(jnp.where(mine, shift_ref[part, i], 0.0), 1, keepdims=True) for i in range(3)
    )
    first = real + shift
    second = second + shift
    scale = 1.0 / (first * second + imaginary * imaginary)
    a, b, c = (
        jnp.broadcast_to(factor * scale, (SLOTS, NODES)) for factor in (second, imaginary, first)
    )

    def apply(value):
        real, imag = value[:SLOTS], value[SLOTS:]
        return jnp.concatenate([a * real + b * imag, c * imag - b * real], 0)

    return apply


def rows_of(part):
    return slice(part * ROWS, (part + 1) * ROWS)


def first_kernel(part, rates_ref, here_ref, series_ref, high_ref, low_ref, shift_ref, spec_ref, out_ref):
    apply = solved(here_ref, shift_ref, part, STEP_SCALE * rates_ref[0])
    mine = here_ref[0] // 2
    high, low = high_ref[mine, rows_of(part)], low_ref[mine, rows_of(part)]
    for e in range(PLANE):
        spec = table_product(high, low, series_ref[e])
        spec_ref[e] = spec
        out_ref[e] = apply(spec)


def folded(product):
    return (product[:ROWS, :NODES] + product[:ROWS, NODES:]) + (
        product[ROWS:, :NODES] + product[ROWS:, NODES:]
    )


def near_kernel(
    part, sweep, rates_ref, here_ref, nb_ref, y_ref, pair_ref, spec_ref, weights_ref, out_ref, split_ref
):
    core = here_ref[0] % 2
    keep = STEP_SCALE * rates_ref[sweep] - STEP_SCALE * DIAG_WEIGHT
    for place, ref in enumerate((y_ref, pair_ref)):
        for e in range(PLANE):
            high, low = split(ref[e])
            split_ref[place * PLANE + e, :ROWS] = high
            split_ref[place * PLANE + e, ROWS:] = low
    for e in range(PLANE):
        picked = [nb_ref[e, s] % PLANE for s in OWN_SLOTS] + [PLANE + jnp.where(core == 0, nb_ref[e, 2], nb_ref[e, 1]) % PLANE]
        product = dot(jnp.concatenate([split_ref[i] for i in picked], 1), weights_ref[e])
        out_ref[e] = (
            spec_ref[e]
            + keep * y_ref[e]
            - (STEP_SCALE * BLOCK_WEIGHT) * folded(product)
        )


def far_kernel(part, sweep, rates_ref, here_ref, nb_ref, base_ref, far_ref, shift_ref, weights_ref, *rest):
    core = here_ref[0] % 2
    apply = solved(here_ref, shift_ref, part, STEP_SCALE * rates_ref[sweep])
    out_ref = rest[-1]
    for e in range(PLANE):
        picked = jnp.where(core == 0, nb_ref[e, 1], nb_ref[e, 2]) % PLANE
        product = dot(jnp.concatenate(split(far_ref[picked]), 0), weights_ref[e])
        result = apply(base_ref[e] - (STEP_SCALE * BLOCK_WEIGHT) * folded(product))
        if len(rest) == 1:
            out_ref[e] = result
        else:
            for other in range(PARTS - 1):
                out_ref[e, rows_of(other)] = rest[other][e]
            out_ref[e, rows_of(part)] = result


def whole(count):
    return [pl.BlockSpec(memory_space=pltpu.VMEM)] * count


def call(kernel, outs, specs, flops, moved, scratch=()):
    return pl.pallas_call(
        kernel,
        out_shape=outs,
        in_specs=specs,
        out_specs=jax.tree.map(lambda _: pl.BlockSpec(memory_space=pltpu.VMEM), outs),
        scratch_shapes=scratch,
        compiler_params=pltpu.CompilerParams(vmem_limit_bytes=VMEM_LIMIT),
        cost_estimate=pl.CostEstimate(flops=flops, bytes_accessed=moved, transcendentals=0),
    )


STEPS = jax.ShapeDtypeStruct((PLANE, 2 * HALF, NODES), jnp.float32)
STATE = jax.ShapeDtypeStruct((PLANE, ROWS, NODES), jnp.float32)
MIB = 1 << 20


def per_device(right_side, blocks, neighbors, shift_rates):
    forward, inverse = transform_tables()
    forward_high, forward_low = (jnp.asarray(part) for part in split_host(forward))
    inverse_high, inverse_low = (jnp.asarray(part) for part in split_host(inverse))
    shifts = jnp.asarray(shift_table())
    here = (lax.axis_index("tm") * 2 + (lax.axis_index("space") & 1)).astype(jnp.int32).reshape(1)
    right_side, here = lax.optimization_barrier((right_side, here))
    ring = lax.axis_size("space")
    on_chip = [(i, i ^ 1) for i in range(ring)]
    groups = [[p * ring + place for p in ORDERS[place % 2]] for place in range(ring)]
    off_chip = [(i, (i + 1 if i % 2 else i - 1) % ring) for i in range(ring)]

    def exchange(value):
        return lax.all_to_all(
            value, ("tm", "space"), 0, 0, tiled=True, axis_index_groups=groups
        )

    series = exchange(call(forward_kernel, STEPS, whole(2), 0, 2 * MIB)(here, exchange(right_side)))
    spectrum, states = zip(
        *(
            call(
                functools.partial(first_kernel, part),
                (STATE, STATE),
                whole(6),
                10**9 // PARTS,
                4 * MIB // PARTS,
            )(shift_rates, here, series, forward_high, forward_low, shifts)
            for part in range(PARTS)
        )
    )
    states = list(states)
    near_weights, far_weights = call(
        weights_kernel,
        (
            jax.ShapeDtypeStruct((PLANE, 6 * NODES, 2 * NODES), jnp.bfloat16),
            jax.ShapeDtypeStruct((PLANE, NODES, 2 * NODES), jnp.bfloat16),
        ),
        whole(2) + [pl.BlockSpec(memory_space=pl.ANY)],
        0,
        8 * MIB,
    )(here, blocks, states[0])
    for sweep in range(1, SWEEPS):
        for part in range(PARTS):
            state = states[part]
            pair = lax.ppermute(state, "space", on_chip)
            far = lax.ppermute(state, "space", off_chip)
            base = call(
                functools.partial(near_kernel, part, sweep),
                STATE,
                whole(7),
                2 * 10**9 // PARTS,
                5 * MIB // PARTS,
                [pltpu.VMEM((2 * PLANE, 2 * ROWS, NODES), jnp.bfloat16)],
            )(shift_rates, here, neighbors, state, pair, spectrum[part], near_weights)
            last = sweep == SWEEPS - 1 and part == PARTS - 1
            others = states[: PARTS - 1] if last else []
            states[part] = call(
                functools.partial(far_kernel, part, sweep),
                STEPS if last else STATE,
                whole(7 + len(others)),
                10**9 // PARTS,
                3 * MIB // PARTS,
            )(shift_rates, here, neighbors, base, far, shifts, far_weights, *others)
    steps = call(
        inverse_kernel,
        STEPS,
        whole(4),
        10**9,
        4 * MIB,
        [pltpu.VMEM((CLASSES, 256, NODES), jnp.float32)],
    )(here, exchange(states[-1]), inverse_high, inverse_low)
    return exchange(steps)


def solution(mesh):
    return jax.shard_map(
        per_device,
        mesh=mesh,
        in_specs=(P("space", "tm", None), P("space", None, None, None), P("space", None), P()),
        out_specs=P("space", "tm", None),
        check_vma=False,
    )
```

```python
import functools
import math

import jax
import jax.numpy as jnp
import numpy as np
from jax import lax
from jax.experimental import pallas as pl
from jax.experimental.pallas import tpu as pltpu
from jax.sharding import PartitionSpec as P

SWEEPS = 4
LENGTH = 2048
CLASSES = 8
HALF = 128
PARTS = 2
SLOTS = HALF // PARTS
ROWS = 2 * SLOTS
NODES = 128
PLANE = 8
WRAP_WEIGHT = 0.01
DIAG_WEIGHT = 6.0
BLOCK_WEIGHT = 3.0
STEP_SCALE = 0.1
OWN_SLOTS = (0, 3, 4, 5, 6)
ROOT2 = math.sqrt(0.5)
VMEM_LIMIT = 16 * 1024 * 1024


def slot_frequencies(c):
    j = np.arange(HALF)
    return 8 * j if c == 0 else c + 16 * j


def transform_tables():
    m = np.arange(HALF)
    log_g = math.log(WRAP_WEIGHT) / LENGTH
    forward = np.zeros((CLASSES, 256, 256))
    inverse = np.zeros((CLASSES, 256, 256))
    for c in range(CLASSES):
        k = slot_frequencies(c)
        angle = 2.0 * np.pi * ((k[:, None] * m[None, :]) % LENGTH) / LENGTH
        cos, sin = np.cos(angle), np.sin(angle)
        if c:
            forward[c] = np.block([[cos, sin], [-sin, cos]])
            inverse[c] = np.block([[cos.T, -sin.T], [sin.T, cos.T]]) * (2.0 / LENGTH)
        else:
            even = (np.arange(HALF) % 2 == 0)[:, None]
            sign = np.where(m % 2 == 0, 1.0, -1.0)
            cos_even, cos_odd = cos * even, cos * ~even
            sin_even, sin_odd = sin * even, sin * ~even
            forward[c] = np.block([[cos_even, cos_odd], [-sin_even, -sin_odd]])
            forward[c, HALF, :HALF] = sign
            back = np.block([[cos_even.T, -sin_even.T], [cos_odd.T, -sin_odd.T]]) * (2.0 / LENGTH)
            back[:HALF, 0] = 1.0 / LENGTH
            back[:HALF, HALF] = sign / LENGTH
            inverse[c] = back
    growth = np.exp(log_g * m)
    forward *= np.tile(growth, 2)[None, None, :]
    inverse /= np.tile(growth, 2)[None, :, None]
    order = np.arange(256).reshape(2, PARTS, SLOTS).transpose(1, 0, 2).reshape(256)
    return forward[:, order], inverse[:, :, order]


def shift_table():
    root = math.exp(math.log(WRAP_WEIGHT) / LENGTH)
    table = np.zeros((3, HALF, NODES))
    for c in range(CLASSES):
        angle = 2.0 * np.pi * slot_frequencies(c) / LENGTH
        real = 1.0 - root * np.cos(angle)
        second = real.copy()
        if c == 0:
            second[0] = 1.0 + root
        table[0, :, c] = real
        table[1, :, c] = second
        table[2, :, c] = root * np.sin(angle)
    return table.reshape(3, PARTS, SLOTS, NODES).transpose(1, 0, 2, 3).astype(np.float32)


def split_host(matrix):
    high = matrix.astype(jnp.bfloat16)
    low = (matrix - high.astype(np.float64)).astype(jnp.bfloat16)
    return high, low


def split(value):
    high = value.astype(jnp.bfloat16)
    return high, (value - high.astype(jnp.float32)).astype(jnp.bfloat16)


def dot(a, b):
    return jnp.dot(a, b, preferred_element_type=jnp.float32)


BLOCK_GROWTH = [math.exp(math.log(WRAP_WEIGHT) * q / 16.0) for q in range(16)]


def real_dft16(s):
    u = [s[r] + s[r + 8] for r in range(8)]
    w = [s[r] - s[r + 8] for r in range(8)]
    p = [u[r] + u[r + 4] for r in range(4)]
    t = [u[r] - u[r + 4] for r in range(4)]
    out = [None] * 8
    a, b = p[0] + p[2], p[1] + p[3]
    out[0] = (a + b, a - b)
    out[4] = (p[0] - p[2], p[3] - p[1])
    minus, plus = ROOT2 * (t[1] - t[3]), ROOT2 * (t[1] + t[3])
    out[2] = (t[0] + minus, -t[2] - plus)
    out[6] = (t[0] - minus, t[2] - plus)
    lower = [w[r] - w[8 - r] for r in (1, 2, 3)]
    upper = [w[r] + w[8 - r] for r in (1, 2, 3)]
    for c in (1, 3, 5, 7):
        real = w[0]
        imag = -w[4] if c % 4 == 1 else w[4]
        for r in (1, 2, 3):
            real = real + math.cos(math.pi * c * r / 8) * lower[r - 1]
            imag = imag - math.sin(math.pi * c * r / 8) * upper[r - 1]
        out[c] = (real, imag)
    return out


def real_idft16(v):
    (v0, v8), (r2, i2), (r4, i4), (r6, i6) = v[0], v[2], v[4], v[6]
    a, b = v0 + v8, v0 - v8
    ee = [a + r4, b - i4, a - r4, b + i4]
    x, y = r2 - r6, i2 + i6
    eo = [r2 + r6, ROOT2 * (x - y), i6 - i2, -ROOT2 * (x + y)]
    even = [ee[q] + eo[q] for q in range(4)] + [ee[q] - eo[q] for q in range(4)]
    odd = [None] * 8
    odd[0] = (v[1][0] + v[3][0]) + (v[5][0] + v[7][0])
    odd[4] = (v[3][1] - v[1][1]) + (v[7][1] - v[5][1])
    for q in (1, 2, 3):
        real = sum(math.cos(math.pi * c * q / 8) * v[c][0] for c in (1, 3, 5, 7))
        imag = sum(math.sin(math.pi * c * q / 8) * v[c][1] for c in (1, 3, 5, 7))
        odd[q] = real - imag
        odd[8 - q] = -real - imag
    return [even[q] + odd[q] for q in range(8)] + [even[q] - odd[q] for q in range(8)]


CHUNK = 16
ORDERS = ((0, 4, 2, 6, 3, 7, 1, 5), (5, 1, 7, 3, 6, 2, 4, 0))


def places_of(here_ref):
    return [
        jnp.where(here_ref[0] % 2 == 0, ORDERS[0].index(p), ORDERS[1].index(p)) for p in range(8)
    ]


def steps_at(places, q, row):
    return places[q // 2], pl.ds(q % 2 * HALF + row, CHUNK), slice(None)


def table_product(high, low, value):
    value_high, value_low = split(value)
    both = dot(high, jnp.concatenate([value_high, value_low], 1))
    return both[:, :NODES] + both[:, NODES:] + dot(low, value_high)


def forward_kernel(here_ref, x_ref, out_ref):
    places = places_of(here_ref)

    @pl.loop(0, HALF // CHUNK, unroll=True)
    def _(step):
        row = pl.multiple_of(step * CHUNK, CHUNK)
        series = [x_ref[steps_at(places, q, row)] * BLOCK_GROWTH[q] for q in range(16)]
        for c, (real, imag) in enumerate(real_dft16(series)):
            out_ref[places[c], pl.ds(row, CHUNK), :] = real
            out_ref[places[c], pl.ds(HALF + row, CHUNK), :] = imag


def inverse_kernel(here_ref, y_ref, high_ref, low_ref, out_ref, v_ref):
    places = places_of(here_ref)
    for c in range(CLASSES):
        v_ref[c] = table_product(high_ref[c], low_ref[c], y_ref[places[c]])

    @pl.loop(0, HALF // CHUNK, unroll=True)
    def _(step):
        row = pl.multiple_of(step * CHUNK, CHUNK)
        pairs = [
            (v_ref[c, pl.ds(row, CHUNK), :], v_ref[c, pl.ds(HALF + row, CHUNK), :])
            for c in range(CLASSES)
        ]
        for q, value in enumerate(real_idft16(pairs)):
            out_ref[steps_at(places, q, row)] = value * (1.0 / BLOCK_GROWTH[q])


def weights_kernel(here_ref, blocks_ref, _, near_ref, far_ref):
    core = here_ref[0] % 2
    for e in range(PLANE):
        for place, s in enumerate(OWN_SLOTS + (2 - core,)):
            high, low = split(blocks_ref[e, s].T)
            near_ref[e, place * NODES : (place + 1) * NODES, :NODES] = high
            near_ref[e, place * NODES : (place + 1) * NODES, NODES:] = low
        high, low = split(blocks_ref[e, 1 + core].T)
        far_ref[e, :, :NODES] = high
        far_ref[e, :, NODES:] = low


def solved(here_ref, shift_ref, part, shift):
    mine = lax.broadcasted_iota(jnp.int32, (SLOTS, NODES), 1) == here_ref[0] // 2
    real, second, imaginary = (
        jnp.sum(jnp.where(mine, shift_ref[part, i], 0.0), 1, keepdims=True) for i in range(3)
    )
    first = real + shift
    second = second + shift
    scale = 1.0 / (first * second + imaginary * imaginary)
    a, b, c = (
        jnp.broadcast_to(factor * scale, (SLOTS, NODES)) for factor in (second, imaginary, first)
    )

    def apply(value):
        real, imag = value[:SLOTS], value[SLOTS:]
        return jnp.concatenate([a * real + b * imag, c * imag - b * real], 0)

    return apply


def rows_of(part):
    return slice(part * ROWS, (part + 1) * ROWS)


def first_kernel(part, rates_ref, here_ref, series_ref, high_ref, low_ref, shift_ref, spec_ref, out_ref):
    apply = solved(here_ref, shift_ref, part, STEP_SCALE * rates_ref[0])
    mine = here_ref[0] // 2
    high, low = high_ref[mine, rows_of(part)], low_ref[mine, rows_of(part)]
    for e in range(PLANE):
        spec = table_product(high, low, series_ref[e])
        spec_ref[e] = spec
        out_ref[e] = apply(spec)


def folded(product):
    return (product[:ROWS, :NODES] + product[:ROWS, NODES:]) + (
        product[ROWS:, :NODES] + product[ROWS:, NODES:]
    )


def near_kernel(
    part, sweep, rates_ref, here_ref, nb_ref, y_ref, pair_ref, spec_ref, weights_ref, out_ref, split_ref
):
    core = here_ref[0] % 2
    keep = STEP_SCALE * rates_ref[sweep] - STEP_SCALE * DIAG_WEIGHT
    for place, ref in enumerate((y_ref, pair_ref)):
        for e in range(PLANE):
            high, low = split(ref[e])
            split_ref[place * PLANE + e, :ROWS] = high
            split_ref[place * PLANE + e, ROWS:] = low
    for e in range(PLANE):
        picked = [nb_ref[e, s] % PLANE for s in OWN_SLOTS] + [PLANE + jnp.where(core == 0, nb_ref[e, 2], nb_ref[e, 1]) % PLANE]
        product = dot(jnp.concatenate([split_ref[i] for i in picked], 1), weights_ref[e])
        out_ref[e] = (
            spec_ref[e]
            + keep * y_ref[e]
            - (STEP_SCALE * BLOCK_WEIGHT) * folded(product)
        )


def far_kernel(part, sweep, rates_ref, here_ref, nb_ref, base_ref, far_ref, shift_ref, weights_ref, *rest):
    core = here_ref[0] % 2
    apply = solved(here_ref, shift_ref, part, STEP_SCALE * rates_ref[sweep])
    out_ref = rest[-1]
    for e in range(PLANE):
        picked = jnp.where(core == 0, nb_ref[e, 1], nb_ref[e, 2]) % PLANE
        product = dot(jnp.concatenate(split(far_ref[picked]), 0), weights_ref[e])
        result = apply(base_ref[e] - (STEP_SCALE * BLOCK_WEIGHT) * folded(product))
        if len(rest) == 1:
            out_ref[e] = result
        else:
            for other in range(PARTS - 1):
                out_ref[e, rows_of(other)] = rest[other][e]
            out_ref[e, rows_of(part)] = result


def whole(count):
    return [pl.BlockSpec(memory_space=pltpu.VMEM)] * count


def call(kernel, outs, specs, flops, moved, scratch=()):
    return pl.pallas_call(
        kernel,
        out_shape=outs,
        in_specs=specs,
        out_specs=jax.tree.map(lambda _: pl.BlockSpec(memory_space=pltpu.VMEM), outs),
        scratch_shapes=scratch,
        compiler_params=pltpu.CompilerParams(vmem_limit_bytes=VMEM_LIMIT),
        cost_estimate=pl.CostEstimate(flops=flops, bytes_accessed=moved, transcendentals=0),
    )


STEPS = jax.ShapeDtypeStruct((PLANE, 2 * HALF, NODES), jnp.float32)
STATE = jax.ShapeDtypeStruct((PLANE, ROWS, NODES), jnp.float32)
MIB = 1 << 20


def per_device(right_side, blocks, neighbors, shift_rates):
    forward, inverse = transform_tables()
    forward_high, forward_low = (jnp.asarray(part) for part in split_host(forward))
    inverse_high, inverse_low = (jnp.asarray(part) for part in split_host(inverse))
    shifts = jnp.asarray(shift_table())
    here = (lax.axis_index("tm") * 2 + (lax.axis_index("space") & 1)).astype(jnp.int32).reshape(1)
    right_side, here = lax.optimization_barrier((right_side, here))
    ring = lax.axis_size("space")
    on_chip = [(i, i ^ 1) for i in range(ring)]
    groups = [[p * ring + place for p in ORDERS[place % 2]] for place in range(ring)]
    off_chip = [(i, (i + 1 if i % 2 else i - 1) % ring) for i in range(ring)]

    def exchange(value):
        return lax.all_to_all(
            value, ("tm", "space"), 0, 0, tiled=True, axis_index_groups=groups
        )

    series = exchange(call(forward_kernel, STEPS, whole(2), 0, 2 * MIB)(here, exchange(right_side)))
    spectrum, states = zip(
        *(
            call(
                functools.partial(first_kernel, part),
                (STATE, STATE),
                whole(6),
                10**9 // PARTS,
                4 * MIB // PARTS,
            )(shift_rates, here, series, forward_high, forward_low, shifts)
            for part in range(PARTS)
        )
    )
    states = list(states)
    near_weights, far_weights = call(
        weights_kernel,
        (
            jax.ShapeDtypeStruct((PLANE, 6 * NODES, 2 * NODES), jnp.bfloat16),
            jax.ShapeDtypeStruct((PLANE, NODES, 2 * NODES), jnp.bfloat16),
        ),
        whole(2) + [pl.BlockSpec(memory_space=pl.ANY)],
        0,
        8 * MIB,
    )(here, blocks, states[0])
    for sweep in range(1, SWEEPS):
        for part in range(PARTS):
            state = states[part]
            pair = lax.ppermute(state, "space", on_chip)
            far = lax.ppermute(state, "space", off_chip)
            base = call(
                functools.partial(near_kernel, part, sweep),
                STATE,
                whole(7),
                2 * 10**9 // PARTS,
                5 * MIB // PARTS,
                [pltpu.VMEM((2 * PLANE, 2 * ROWS, NODES), jnp.bfloat16)],
            )(shift_rates, here, neighbors, state, pair, spectrum[part], near_weights)
            last = sweep == SWEEPS - 1 and part == PARTS - 1
            others = states[: PARTS - 1] if last else []
            states[part] = call(
                functools.partial(far_kernel, part, sweep),
                STEPS if last else STATE,
                whole(7 + len(others)),
                10**9 // PARTS,
                3 * MIB // PARTS,
            )(shift_rates, here, neighbors, base, far, shifts, far_weights, *others)
    steps = call(
        inverse_kernel,
        STEPS,
        whole(4),
        10**9,
        4 * MIB,
        [pltpu.VMEM((CLASSES, 256, NODES), jnp.float32)],
    )(here, exchange(states[-1]), inverse_high, inverse_low)
    return exchange(steps)


def solution(mesh):
    return jax.shard_map(
        per_device,
        mesh=mesh,
        in_specs=(P("space", "tm", None), P("space", None, None, None), P("space", None), P()),
        out_specs=P("space", "tm", None),
        check_vma=False,
    )
```
